32 devices in a mesh: groups: 2 (over y), strip: 4 (over z), section: 2 (over x), col: 2 (over core).
Axes of the slice: x: 2, y: 2, z: 4, core: 2. Of those that a mesh axis runs over, the one named last changes fastest.
Arguments:
- x_in: float32 [8, 512, 16, 256], P('groups', None, 'strip', 'col'), parts along dimension 0, may hold values from -6 to 6
- w_reduce: float32 [2, 128, 512], P('section'), may hold values from -0.25 to 0.25
- w_spatial: float32 [2, 9, 128, 128], P('section'), may hold values from -0.1875 to 0.1875
- w_expand: float32 [2, 512, 128], P('section'), may hold values from -0.5 to 0.5
- gain_mid: float32 [2, 2, 128], P('section'), may hold values from 0.1 to 1.9
- bias_mid: float32 [2, 2, 128], P('section'), may hold values from -3 to 3
- gain_out: float32 [2, 512], P('section'), may hold values from 0.1 to 1.9
- bias_out: float32 [2, 512], P('section'), may hold values from -3 to 3
Outputs:
- features: float32 [2, 8, 512, 16, 256], P('section', 'groups', None, 'strip', 'col'), parts along dimension 1
The draws below stay inside these ranges and needn't reach their ends.
There are 2 independent parts, one for each index of `groups`. The reference program is written for one: setup_inputs(seed, part) draws one part's arguments, and reference() takes and returns one part's arrays. A program takes and returns all parts, laid end to end along the dimension named above; an argument that names none is the same for every part. Nothing has to cross between parts.
All inputs are finite; a program needn't handle non-finite values.
Results may differ from the reference program's by a relative error of at most 0.00015.
Values sent between devices are 32-bit elements; how exact they have to be, the bound alone decides.
No kernel may reach another device: no remote copies, remote signals or barrier semaphores. Data moves between devices by JAX's collectives and lax.ppermute only.
A program may use at most 64 MiB of HBM per device.

```python
import jax
import jax.numpy as jnp
from jax import lax

C = 512
CM = 128
MB = 4
BLOCKS = 2
H = 16
W = 256


def block_levels(key, shape, cuts, low, high):
    factor_of, own = 1.0, jax.random.fold_in(key, 6)
    for axis_at, parts in cuts:
        heights = jnp.exp(jax.random.uniform(jax.random.fold_in(own, axis_at), (parts,), jnp.float32, low / len(cuts), high / len(cuts)))
        factor_of = factor_of * jnp.repeat(heights, shape[axis_at] // parts).reshape([-1 if axis == axis_at else 1 for axis in range(len(shape))])
    return factor_of


def centred(own_key, dims, spread, reach, split=(), dtype=jnp.bfloat16):
    factor_of = block_levels(own_key, dims, split, -0.22, 0.18) if split else 1.0
    drawn = jax.random.normal(own_key, dims, jnp.float32) * spread * factor_of
    return jnp.minimum(jnp.maximum(drawn, -reach), reach).astype(dtype)


def setup_inputs(seed: int = 0, part: int = 0) -> dict:
    key_of = jax.random.split(jax.random.key(seed), 9)
    part_keys = jax.random.split(jax.random.fold_in(key_of[8], part), 9)
    return {
        "x_in": centred(part_keys[0], (MB, C, H, W), 1.0, 6.0, ((2, 4), (3, 2)), jnp.float32),
        "w_reduce": centred(key_of[1], (BLOCKS, CM, C), C ** -0.5, 0.25, ((0, 2),), jnp.float32),
        "w_spatial": centred(key_of[2], (BLOCKS, 9, CM, CM), (9 * CM) ** -0.5, 0.1875, ((0, 2),), jnp.float32),
        "w_expand": centred(key_of[3], (BLOCKS, C, CM), CM ** -0.5, 0.5, ((0, 2),), jnp.float32),
        "gain_mid": jnp.clip(1.0 + 0.18 * jax.random.normal(key_of[4], (BLOCKS, 2, CM), jnp.float32), 0.1, 1.9),
        "bias_mid": centred(key_of[5], (BLOCKS, 2, CM), 0.5, 3.0, ((0, 2),), jnp.float32),
        "gain_out": jnp.clip(1.0 + 0.18 * jax.random.normal(key_of[6], (BLOCKS, C), jnp.float32), 0.1, 1.9),
        "bias_out": centred(key_of[7], (BLOCKS, C), 0.5, 3.0, ((0, 2),), jnp.float32),
    }


def project(weight, field):
    return jnp.einsum("oc,chw->ohw", weight, field, precision=lax.Precision.HIGHEST)


def column(vector):
    return vector[:, None, None]


def bottleneck(image, w_reduce, w_spatial, w_expand, gain_mid, bias_mid, gain_out, bias_out):
    reduced = jax.nn.relu(column(gain_mid[0]) * project(w_reduce, image) + column(bias_mid[0]))
    padded = jnp.pad(reduced, ((0, 0), (1, 1), (1, 1)))
    spatial = jnp.zeros((CM, H, W), jnp.float32)
    for tap in range(9):
        row_off = tap // 3
        col_off = tap % 3
        spatial = spatial + project(w_spatial[tap], padded[:, row_off:row_off + H, col_off:col_off + W])
    middle = jax.nn.relu(column(gain_mid[1]) * spatial + column(bias_mid[1]))
    return jax.nn.relu(image + column(gain_out) * project(w_expand, middle) + column(bias_out))


def reference(x_in, w_reduce, w_spatial, w_expand, gain_mid, bias_mid, gain_out, bias_out):
    def run_tile(image):
        outputs = []
        current = image
        for level in range(BLOCKS):
            current = bottleneck(current, w_reduce[level], w_spatial[level], w_expand[level],
                                 gain_mid[level], bias_mid[level], gain_out[level], bias_out[level])
            outputs.append(current)
        return jnp.stack(outputs)

    per_tile = lax.map(run_tile, x_in)
    return jnp.transpose(per_tile, (1, 0, 2, 3, 4))
```

```python
import functools

import jax
import jax.numpy as jnp
from jax import lax
from jax.experimental import pallas as pl
from jax.experimental.pallas import tpu as pltpu
from jax.sharding import PartitionSpec as P

F32 = jnp.float32
BF16 = jnp.bfloat16
PAD = 8


def split(value):
    high = value.astype(BF16)
    return high, (value - high.astype(F32)).astype(BF16)


def dot(left, right):
    return jnp.dot(left, right, preferred_element_type=F32)


def dot_nt(left, right):
    return lax.dot_general(left, right, (((1,), (1,)), ((), ())), preferred_element_type=F32)


def column_of(row, lanes=128):
    return jnp.concatenate(
        [
            jnp.transpose(jnp.broadcast_to(row[:, at : at + 128], (lanes, 128)))
            for at in range(0, row.shape[1], 128)
        ],
        axis=0,
    )


def pick_first(flags, own, mine, other, store):
    if mine is None:
        store(0, own[0])
        return
    half = own.shape[1] // 2

    @pl.when(flags[0] == 1)
    def _():
        store(0, own[0])

    for core in range(2):

        @pl.when((flags[0] == 0) & (flags[1] == core))
        def _(core=core):
            store(core * half, mine[:half])
            store((1 - core) * half, other[:half])


def load_reduce(flags, own, mine, other, w_high):
    cm = own.shape[1]

    def store(at, rows):
        high, low = split(rows)
        count = rows.shape[0]
        w_high[at : at + count, :] = high
        w_high[cm + at : cm + at + count, :] = low

    pick_first(flags, own, mine, other, store)


def load_terms(flags, own, mine, terms):
    if mine is None:
        terms[...] = own[...]
        return

    @pl.when(flags[0] == 1)
    def _():
        terms[...] = own[...]

    @pl.when(flags[0] == 0)
    def _():
        terms[...] = mine[mine.shape[0] - 8 :, :]


def load_rest(flags, own_spatial, own_expand, mine, other, terms, w_spatial, w_expand):
    cm = own_spatial.shape[2]
    c = own_expand.shape[1]
    half, wide = cm // 2, c // 2
    gain = column_of(terms[1:2, :])

    def store_tap(tap, at, rows):
        turned = jnp.transpose(rows)
        high, low = split(turned)
        count = rows.shape[0]
        w_spatial[tap * cm : (tap + 1) * cm, at : at + count] = high
        w_spatial[tap * cm : (tap + 1) * cm, cm + at : cm + at + count] = low

    def store_expand(at, rows):
        count = rows.shape[0]
        high, low = split(rows * gain[at : at + count])
        w_expand[at : at + count, 0:cm] = high
        w_expand[at : at + count, cm : 2 * cm] = low
        w_expand[at : at + count, 2 * cm : 3 * cm] = high

    def from_own():
        for tap in range(9):
            store_tap(tap, 0, own_spatial[0, tap])
        store_expand(0, own_expand[0])

    if mine is None:
        from_own()
        return

    @pl.when(flags[0] == 1)
    def _():
        from_own()

    for core in range(2):

        @pl.when((flags[0] == 0) & (flags[1] == core))
        def _(core=core):
            low, up = (mine, other) if core == 0 else (other, mine)
            for tap in range(9):
                rows = jnp.concatenate(
                    [low[tap * half : (tap + 1) * half], up[tap * half : (tap + 1) * half]], axis=0
                )
                store_tap(tap, 0, rows)
            store_expand(0, low[9 * half : 9 * half + wide])
            store_expand(wide, up[9 * half : 9 * half + wide])


def reduce_rows(flags, tile, fields, w_reduce, terms, outs):
    r_out, msg_a, msg_b, edge, corner_a, corner_b = outs
    rows = len(fields)
    cols = fields[0].shape[1]
    cm = w_reduce.shape[0] // 2
    parts = [split(field) for field in fields]
    high = jnp.concatenate([part[0] for part in parts], axis=1)
    low = jnp.concatenate([part[1] for part in parts], axis=1)
    both = dot(w_reduce[...], high)
    total = both[:cm] + both[cm:] + dot(w_reduce[:cm, :], low)
    gain = terms[0:1, 0:cm]
    shift = terms[0:1, 2 * cm : 3 * cm]
    turned = [
        jnp.maximum(jnp.transpose(total[:, r * cols : (r + 1) * cols]) * gain + shift, 0.0) for r in range(rows)
    ]
    even, first_core = flags[2] == 0, flags[1] == 0
    edges = []
    for r in range(rows):
        r_out[0, r] = turned[r]
        edges.append(jnp.where(first_core, turned[r][cols - 1 : cols, :], turned[r][0:1, :]))
        edge[0, r : r + 1, :] = edges[r]
    msg_a[0] = jnp.where(even, turned[rows - 1], turned[0])
    msg_b[0] = jnp.where(even, turned[0], turned[rows - 1])
    corner_a[0, 0:1, :] = jnp.where(even, edges[rows - 1], edges[0])
    corner_b[0, 0:1, :] = jnp.where(even, edges[0], edges[rows - 1])


def reduce_kernel(remote, flags, x, own_first, own_terms, *refs):
    mine, other = (refs[0], refs[1]) if remote else (None, None)
    refs = refs[2:] if remote else refs
    outs, (w_reduce, terms) = refs[:6], refs[6:]
    rows = outs[0].shape[1]
    c = own_first.shape[2]
    tile = pl.program_id(0)

    @pl.when(tile == 0)
    def _():
        load_terms(flags, own_terms, mine, terms)
        load_reduce(flags, own_first, mine, other, w_reduce)

    fields = [x[0, pl.ds(r, c, stride=rows), :] for r in range(rows)]
    reduce_rows(flags, tile, fields, w_reduce, terms, outs)


def block_kernel(
    remote, remote_next, last, flags, next_flags, x, r_in, halo_a, halo_b, edge_in, diag_a, diag_b,
    own_spatial, own_expand, own_terms, *refs,
):
    refs = list(refs)
    mine_first, mine, other = (refs.pop(0), refs.pop(0), refs.pop(0)) if remote else (None, None, None)
    if not last:
        own_first = refs.pop(0)
        next_mine, next_other = (refs.pop(0), refs.pop(0)) if remote_next else (None, None)
    out = refs.pop(0)
    outs = [refs.pop(0) for _ in range(6)] if not last else None
    w_spatial, w_expand, terms, shift_out, padded, taps_high, taps_low = refs[:7]
    if not last:
        w_reduce, next_terms = refs[7:]
    rows, cols, cm = r_in.shape[1:]
    c = own_expand.shape[1]
    tile = pl.program_id(0)

    @pl.when(tile == 0)
    def _():
        load_terms(flags, own_terms, mine_first, terms)
        load_rest(flags, own_spatial, own_expand, mine, other, terms, w_spatial, w_expand)
        shift_out[...] = column_of(terms[2:3, :])
        padded[...] = jnp.zeros_like(padded)
        if not last:
            load_terms(next_flags, own_terms, next_mine, next_terms)
            load_reduce(next_flags, own_first, next_mine, next_other, w_reduce)

    even, first_core = flags[2] == 0, flags[1] == 0
    field = padded.at[:, PAD : PAD + cols, :]
    for r in range(rows):
        field[r + 1] = r_in[0, r]
    field[0] = jnp.where(even, halo_b[0], halo_a[0])
    field[rows + 1] = jnp.where(even, halo_a[0], halo_b[0])
    corner_a, corner_b = diag_a[0, 0:1, :], diag_b[0, 0:1, :]
    sides = [jnp.where(even, corner_b, corner_a)]
    sides += [edge_in[0, r : r + 1, :] for r in range(rows)]
    sides += [jnp.where(even, corner_a, corner_b)]
    for i in range(rows + 2):
        padded[i, PAD - 1 : PAD, :] = jnp.where(first_core, 0.0, sides[i])
        padded[i, PAD + cols : PAD + cols + 1, :] = jnp.where(first_core, sides[i], 0.0)
    for i in range(rows + 2):
        for q in range(3):
            high, low = split(padded[i, PAD - 1 + q : PAD - 1 + q + cols, :])
            taps_high[i * cols : (i + 1) * cols, q * cm : (q + 1) * cm] = high
            taps_low[i * cols : (i + 1) * cols, q * cm : (q + 1) * cm] = low

    span = rows * cols
    high = jnp.concatenate([taps_high[p * cols : p * cols + span, :] for p in range(3)], axis=1)
    low = jnp.concatenate([taps_low[p * cols : p * cols + span, :] for p in range(3)], axis=1)
    both = dot(high, w_spatial[...])
    spatial = both[:, :cm] + both[:, cm:] + dot(low, w_spatial[:, :cm])
    gain = terms[0:1, cm : 2 * cm]
    shift = terms[0:1, 3 * cm : 4 * cm]
    middle = jnp.maximum(spatial * gain + shift, 0.0)
    high, low = split(middle)
    branch = dot_nt(w_expand[...], jnp.concatenate([high, high, low], axis=1))
    keep = flags[3] == 1
    fields = []
    for r in range(rows):
        before = x[0, pl.ds(r, c, stride=rows), :]
        after = jnp.maximum(before + branch[:, r * cols : (r + 1) * cols] + shift_out[...], 0.0)
        after = jnp.where(keep, after, before)
        out[0, pl.ds(r, c, stride=rows), :] = after
        fields.append(after)
    if not last:
        reduce_rows(next_flags, tile, fields, w_reduce, next_terms, outs)


def whole(array):
    return pl.BlockSpec(array.shape, lambda t: (0,) * array.ndim)


def per_tile(shape):
    return pl.BlockSpec((1,) + tuple(shape[1:]), lambda t: (t,) + (0,) * (len(shape) - 1))


SMEM = pl.BlockSpec(memory_space=pltpu.SMEM)


def sent_shapes(tiles, rows, cols, cm):
    return [
        (tiles, rows, cols, cm),
        (tiles, cols, cm),
        (tiles, cols, cm),
        (tiles, 8, cm),
        (tiles, 8, cm),
        (tiles, 8, cm),
    ]


def call(kernel, name, tiles, args, specs, shapes, scratch, flops, moved):
    return pl.pallas_call(
        kernel,
        name=name,
        grid=(tiles,),
        in_specs=specs,
        out_specs=[per_tile(shape) for shape in shapes],
        out_shape=[jax.ShapeDtypeStruct(shape, F32) for shape in shapes],
        scratch_shapes=scratch,
        compiler_params=pltpu.CompilerParams(
            vmem_limit_bytes=40 * 2**20, dimension_semantics=("arbitrary",)
        ),
        cost_estimate=pl.CostEstimate(flops=flops, bytes_accessed=moved, transcendentals=0),
    )(*args)


def on_device(x_in, w_reduce, w_spatial, w_expand, gain_mid, bias_mid, gain_out, bias_out):
    sections = lax.axis_size("section")
    strips = lax.axis_size("strip")
    section = lax.axis_index("section")
    strip = lax.axis_index("strip")
    core = lax.axis_index("col")
    tiles, c, rows, cols = x_in.shape
    cm = w_reduce.shape[1]
    half, wide = cm // 2, c // 2

    terms = jnp.concatenate(
        [
            jnp.concatenate([gain_mid.reshape(1, 2 * cm), bias_mid.reshape(1, 2 * cm)], axis=1),
            gain_out,
            bias_out,
            jnp.zeros((5, c), F32),
        ],
        axis=0,
    )
    first = jnp.concatenate([lax.dynamic_slice_in_dim(w_reduce[0], core * half, half, 0), terms], axis=0)
    rest = jnp.concatenate(
        [
            lax.dynamic_slice_in_dim(w_spatial[0], core * half, half, 1).reshape(9 * half, cm),
            lax.dynamic_slice_in_dim(w_expand[0], core * wide, wide, 0),
        ],
        axis=0,
    )

    def swap(array):
        return lax.ppermute(array, "col", [(0, 1), (1, 0)])

    def from_section(array, level):
        total = None
        for step in range(1, sections - level):
            sent = lax.ppermute(array, "section", [(i, i + step) for i in range(sections - step)])
            total = sent if total is None else jnp.where(section - level == step, sent, total)
        return total

    firsts, rests = {}, {}
    for level in range(sections - 1):
        mine = from_section(first, level)
        firsts[level] = (mine, swap(mine))
        mine = from_section(rest, level)
        rests[level] = (mine, swap(mine))

    def flags_of(level):
        return jnp.stack(
            [
                (section == level).astype(jnp.int32),
                core.astype(jnp.int32),
                (strip % 2).astype(jnp.int32),
                (section >= level).astype(jnp.int32),
            ]
        )

    def pairs(start, cross):
        found = []
        for i in range(start, strips - 1, 2):
            for side in range(2):
                there = 1 - side if cross else side
                found += [(2 * i + side, 2 * (i + 1) + there), (2 * (i + 1) + there, 2 * i + side)]
        return found

    def exchange(sent):
        r, msg_a, msg_b, edge, corner_a, corner_b = sent
        axes = ("strip", "col")
        return (
            r,
            lax.ppermute(msg_a, axes, pairs(0, False)),
            lax.ppermute(msg_b, axes, pairs(1, False)),
            swap(edge),
            lax.ppermute(corner_a, axes, pairs(0, True)),
            lax.ppermute(corner_b, axes, pairs(1, True)),
        )

    flat = x_in.reshape(tiles, c * rows, cols)
    sent = sent_shapes(tiles, rows, cols, cm)
    cells = tiles * rows * cols
    reduce_scratch = [pltpu.VMEM((2 * cm, c), BF16), pltpu.VMEM((8, c), F32)]
    block_scratch = [
        pltpu.VMEM((9 * cm, 2 * cm), BF16),
        pltpu.VMEM((c, 3 * cm), BF16),
        pltpu.VMEM((8, c), F32),
        pltpu.VMEM((c, cols), F32),
        pltpu.VMEM((rows + 2, cols + 2 * PAD, cm), F32),
        pltpu.VMEM(((rows + 2) * cols, 3 * cm), BF16),
        pltpu.VMEM(((rows + 2) * cols, 3 * cm), BF16),
    ]

    args = [flags_of(0), flat, w_reduce, terms]
    specs = [SMEM, per_tile(flat.shape), whole(w_reduce), whole(terms)]
    if sections > 1:
        args += list(firsts[0])
        specs += [whole(array) for array in firsts[0]]
    outs = call(
        functools.partial(reduce_kernel, sections > 1), "reduce", tiles, args, specs, sent, reduce_scratch,
        6 * cells * c * cm, 4 * cells * (c + cm),
    )
    current = flat
    for level in range(sections):
        last = level == sections - 1
        r, halo_a, halo_b, edge, corner_a, corner_b = exchange(outs)
        remote, remote_next = level < sections - 1, level + 1 < sections - 1
        args = [flags_of(level), flags_of(level + 1), current, r, halo_a, halo_b, edge, corner_a, corner_b]
        specs = [SMEM, SMEM] + [per_tile(array.shape) for array in args[2:]]
        more = [w_spatial, w_expand, terms]
        if remote:
            more += [firsts[level][0]] + list(rests[level])
        if not last:
            more += [w_reduce]
            if remote_next:
                more += list(firsts[level + 1])
        args += more
        specs += [whole(array) for array in more]
        shapes = [flat.shape] + ([] if last else sent)
        outs = call(
            functools.partial(block_kernel, remote, remote_next, last), "block", tiles, args, specs, shapes,
            block_scratch + ([] if last else reduce_scratch),
            6 * cells * (10 * c * cm // 4 + c * cm), 4 * cells * (2 * c + cm),
        )
        current, outs = outs[0], outs[1:]
    return current.reshape(1, tiles, c, rows, cols)


def solution(mesh):
    in_specs = (
        P("groups", None, "strip", "col"),
        P("section", None, None),
        P("section", None, None, None),
        P("section", None, None),
        P("section", None, None),
        P("section", None, None),
        P("section", None),
        P("section", None),
    )
    out_specs = P("section", "groups", None, "strip", "col")
    return jax.shard_map(
        on_device, mesh=mesh, in_specs=in_specs, out_specs=out_specs, check_vma=False
    )
```

```python
import functools

import jax
import jax.numpy as jnp
from jax import lax
from jax.experimental import pallas as pl
from jax.experimental.pallas import tpu as pltpu
from jax.sharding import PartitionSpec as P

F32 = jnp.float32
BF16 = jnp.bfloat16
PAD = 8


def split(value):
    high = value.astype(BF16)
    return high, (value - high.astype(F32)).astype(BF16)


def dot(left, right):
    return jnp.dot(left, right, preferred_element_type=F32)


def dot_nt(left, right):
    return lax.dot_general(left, right, (((1,), (1,)), ((), ())), preferred_element_type=F32)


def first_core():
    return lax.axis_index("col") == 0


def even_strip():
    return lax.axis_index("strip") % 2 == 0


def column_of(row):
    return jnp.concatenate(
        [
            jnp.transpose(jnp.broadcast_to(row[:, at : at + 128], (128, 128)))
            for at in range(0, row.shape[1], 128)
        ],
        axis=0,
    )


def pack_first_kernel(
    w_reduce, gain_mid, bias_mid, gain_out, bias_out, first, gain_held, bias_held, gain_row, bias_row, sem
):
    half = w_reduce.shape[1] // 2
    cm = gain_mid.shape[2]
    start = pl.multiple_of(lax.axis_index("col") * half, half)
    moves = [
        (w_reduce.at[0, pl.ds(start, half), :], first.at[:half, :]),
        (gain_mid.at[0], gain_held),
        (bias_mid.at[0], bias_held),
        (gain_out, gain_row),
        (bias_out, bias_row),
    ]
    copies = [pltpu.make_async_copy(here, there, sem.at[i]) for i, (here, there) in enumerate(moves)]
    for copy in copies:
        copy.start()
    first[half : half + 8, :] = jnp.zeros((8, first.shape[1]), F32)
    for copy in copies:
        copy.wait()
    for i in range(2):
        first[half : half + 1, i * cm : (i + 1) * cm] = gain_held[i : i + 1, :]
        first[half : half + 1, (2 + i) * cm : (3 + i) * cm] = bias_held[i : i + 1, :]
    first[half + 1 : half + 2, :] = gain_row[...]
    first[half + 2 : half + 3, :] = bias_row[...]


def pack_rest_kernel(w_spatial, w_expand, rest, sem):
    half = w_spatial.shape[2] // 2
    wide = w_expand.shape[1] // 2
    low = pl.multiple_of(lax.axis_index("col") * half, half)
    at = pl.multiple_of(lax.axis_index("col") * wide, wide)
    copies = [
        pltpu.make_async_copy(
            w_spatial.at[0, tap, pl.ds(low, half), :], rest.at[tap * half : (tap + 1) * half, :], sem.at[tap]
        )
        for tap in range(9)
    ]
    copies.append(
        pltpu.make_async_copy(w_expand.at[0, pl.ds(at, wide), :], rest.at[9 * half :, :], sem.at[9])
    )
    for copy in copies:
        copy.start()
    for copy in copies:
        copy.wait()


def fetch_kernel(x, held, sem):
    copies = [pltpu.make_async_copy(x.at[t], held.at[t], sem.at[t]) for t in range(x.shape[0])]
    for copy in copies:
        copy.start()
    for copy in copies:
        copy.wait()


def store_reduce(w_high, at, rows):
    cm = w_high.shape[0] // 2
    high, low = split(rows)
    w_high[at : at + rows.shape[0], :] = high
    w_high[cm + at : cm + at + rows.shape[0], :] = low


def store_rest(tap_rows, expand_rows, gain_out, w_spatial, w_expand):
    cm = w_expand.shape[1] // 3
    for tap in range(9):
        high, low = split(jnp.transpose(tap_rows(tap)))
        w_spatial[tap * cm : (tap + 1) * cm, :cm] = high
        w_spatial[tap * cm : (tap + 1) * cm, cm:] = low
    high, low = split(expand_rows * column_of(gain_out))
    w_expand[:, :cm] = high
    w_expand[:, cm : 2 * cm] = low
    w_expand[:, 2 * cm :] = high


def prepare_own_kernel(w_reduce, w_spatial, w_expand, first, out_reduce, out_spatial, out_expand, out_shift, out_terms):
    half = w_reduce.shape[1] // 2
    store_reduce(out_reduce, 0, w_reduce[0])
    terms = first[half : half + 8, :]
    out_terms[...] = terms
    out_shift[...] = column_of(terms[2:3, :])
    store_rest(lambda tap: w_spatial[0, tap], w_expand[0], terms[1:2, :], out_spatial, out_expand)


def prepare_reduce_kernel(level, mine, other, own_reduce, own_terms, out_reduce, out_terms):
    half = mine.shape[0] - 8

    @pl.when(lax.axis_index("section") == level)
    def _():
        out_reduce[...] = own_reduce[...]
        out_terms[...] = own_terms[...]

    @pl.when(lax.axis_index("section") != level)
    def _():
        out_terms[...] = mine[half:, :]
        for core in range(2):

            @pl.when(lax.axis_index("col") == core)
            def _(core=core):
                store_reduce(out_reduce, core * half, mine[:half, :])
                store_reduce(out_reduce, (1 - core) * half, other[:half, :])


def prepare_rest_kernel(
    level, mine, other, terms, own_spatial, own_expand, own_shift, out_spatial, out_expand, out_shift
):
    cm = own_expand.shape[1] // 3
    half, wide = cm // 2, own_expand.shape[0] // 2

    @pl.when(lax.axis_index("section") == level)
    def _():
        out_spatial[...] = own_spatial[...]
        out_expand[...] = own_expand[...]
        out_shift[...] = own_shift[...]

    @pl.when(lax.axis_index("section") != level)
    def _():
        out_shift[...] = column_of(terms[2:3, :])
        for core in range(2):

            @pl.when(lax.axis_index("col") == core)
            def _(core=core):
                low, up = (mine, other) if core == 0 else (other, mine)

                def tap_rows(tap):
                    at = slice(tap * half, (tap + 1) * half)
                    return jnp.concatenate([low[at, :], up[at, :]], axis=0)

                expand = jnp.concatenate([low[9 * half :, :], up[9 * half :, :]], axis=0)
                store_rest(tap_rows, expand, terms[1:2, :], out_spatial, out_expand)


def members(kind, rows):
    return (0, rows - 1) if kind == "border" else tuple(range(1, rows - 1))


def reduce_step(tile, field, w_reduce, terms, r_out, edge, msgs):
    cm = w_reduce.shape[0] // 2
    count, cols = r_out.shape[1:3]
    high, low = split(field)
    both = dot(w_reduce[...], high)
    total = both[:cm] + both[cm:] + dot(w_reduce[:cm, :], low)
    gain, shift = terms[0:1, 0:cm], terms[0:1, 2 * cm : 3 * cm]
    even, first = even_strip(), first_core()
    turned = []
    for j in range(count):
        part = jnp.maximum(jnp.transpose(total[:, j * cols : (j + 1) * cols]) * gain + shift, 0.0)
        r_out[tile, j] = part
        at = tile * count + j
        edge[at : at + 1, :] = jnp.where(first, part[cols - 1 : cols, :], part[0:1, :])
        turned.append(part)
    if msgs:
        msgs[0][tile] = jnp.where(even, turned[-1], turned[0])
        msgs[1][tile] = jnp.where(even, turned[0], turned[-1])


def field_rows(x, kind, rows, tile, j):
    if len(x.shape) == 3:
        return x[tile, pl.ds(members(kind, rows)[j], x.shape[1] // rows, stride=rows), :]
    return x[tile, j]


def bring(x, held, sem, start):
    copies = [pltpu.make_async_copy(x.at[t], held.at[t], sem.at[t]) for t in range(x.shape[0])]
    if start:
        for copy in copies:
            copy.start()
    return copies


def reduce_kernel(kind, rows, x, w_reduce, terms, r_out, edge, *refs):
    msgs, copies = refs, None
    if kind == "inner":
        msgs = ()
        copies = bring(x, *refs, True)
        x = refs[0]
    edge[...] = jnp.zeros_like(edge)
    count = r_out.shape[1]
    for tile in range(x.shape[0]):
        if copies:
            copies[tile].wait()
        field = jnp.concatenate([field_rows(x, kind, rows, tile, j) for j in range(count)], axis=1)
        reduce_step(tile, field, w_reduce, terms, r_out, edge, msgs)


def block_kernel(kind, rows, level, last, *refs):
    refs = list(refs)

    def take(n):
        taken, refs[:n] = refs[:n], []
        return taken

    border = kind == "border"
    x, r_border, r_inner, edge_border, edge_inner = take(5)
    if border:
        halo_a, halo_b, corners = take(3)
    w_spatial, w_expand, shift_out, terms = take(4)
    if not last:
        next_reduce, next_terms = take(2)
    if last and border:
        take(1)
    else:
        take(1)
    outs = take(2 if last and border else 1)
    if not last:
        r_out, edge_out = take(2)
        msgs = take(2) if border else []
        edge_out[...] = jnp.zeros_like(edge_out)
    padded, taps_high, taps_low = take(3)
    copies = None
    if len(x.shape) == 3:
        x_held, x_sem = take(2)
        copies = bring(x, x_held, x_sem, True)
        x = x_held
    tiles, _, cols, cm = r_border.shape
    chosen = members(kind, rows)
    count = len(chosen)
    inner = members("inner", rows)
    even, first = even_strip(), first_core()
    gain, shift = terms[0:1, cm : 2 * cm], terms[0:1, 3 * cm : 4 * cm]
    keep = lax.axis_index("section") >= level

    def row_and_side(tile, i):
        if i in (-1, rows):
            from_a = even if i == rows else jnp.logical_not(even)
            side_a, side_b = corners[tile : tile + 1, :], corners[tiles + tile : tiles + tile + 1, :]
            return jnp.where(from_a, halo_a[tile], halo_b[tile]), jnp.where(from_a, side_a, side_b)
        if i in (0, rows - 1):
            j = 0 if i == 0 else 1
            return r_border[tile, j], edge_border[2 * tile + j : 2 * tile + j + 1, :]
        j = inner.index(i)
        at = tile * len(inner) + j
        return r_inner[tile, j], edge_inner[at : at + 1, :]

    span = count * cols
    for tile in range(tiles):
        for i in sorted({r + p for r in chosen for p in (-1, 0, 1)}):
            field, side = row_and_side(tile, i)
            slot = padded.at[tile, i + 1]
            slot[PAD : PAD + cols, :] = field
            slot[PAD - 1 : PAD, :] = jnp.where(first, 0.0, side)
            slot[PAD + cols : PAD + cols + 1, :] = jnp.where(first, side, 0.0)
            for q in range(3):
                high, low = split(field if q == 1 else slot[PAD - 1 + q : PAD - 1 + q + cols, :])
                for j, r in enumerate(chosen):
                    p = i - r + 1
                    if 0 <= p <= 2:
                        lanes = slice((3 * p + q) * cm, (3 * p + q + 1) * cm)
                        at = (tile * count + j) * cols
                        taps_high[at : at + cols, lanes] = high
                        taps_low[at : at + cols, lanes] = low
    group = 4
    middles = []
    for g in range(0, tiles, group):
        at = slice(g * span, (g + group) * span)
        both = dot(taps_high[at, :], w_spatial[...])
        spatial = both[:, :cm] + both[:, cm:] + dot(taps_low[at, :], w_spatial[:, :cm])
        high, low = split(jnp.maximum(spatial * gain + shift, 0.0))
        middles.append(jnp.concatenate([high, high, low], axis=1))
    for tile in range(tiles):
        g, k = tile // group, tile % group
        branch = dot_nt(w_expand[...], middles[g][k * span : (k + 1) * span])
        after = []
        if copies:
            copies[tile].wait()
        for j in range(count):
            before = field_rows(x, kind, rows, tile, j)
            new = jnp.maximum(before + branch[:, j * cols : (j + 1) * cols] + shift_out[...], 0.0)
            after.append(jnp.where(keep, new, before))
            if last:
                whole = outs[-1]
                whole[tile, pl.ds(chosen[j], whole.shape[1] // rows, stride=rows), :] = after[j]
            else:
                outs[0][tile, j] = after[j]
        if not last:
            field = jnp.concatenate(after, axis=1)
            reduce_step(tile, field, next_reduce, next_terms, r_out, edge_out, msgs)
        if last and border:
            sem = refs[0]
            pltpu.make_async_copy(outs[1].at[tile], outs[0].at[tile], sem.at[tile]).start()
    if last and border:
        sem = refs[0]
        for tile in range(tiles):
            pltpu.make_async_copy(outs[1].at[tile], outs[0].at[tile], sem.at[tile]).wait()


VMEM = pl.BlockSpec(memory_space=pltpu.VMEM)
ANY = pl.BlockSpec(memory_space=pl.ANY)
HBM = pl.BlockSpec(memory_space=pl.ANY)
FAR = pl.BlockSpec(memory_space=pltpu.VMEM)


def near(shape, dtype=F32):
    return pltpu.VMEM(shape, dtype)


def call(kernel, name, args, outs, scratch=(), flops=0, moved=0, specs=None, out_specs=None, aliases=None):
    held = {id(VMEM): pltpu.VMEM, id(HBM): pltpu.HBM, id(FAR): pltpu.HBM}
    arrays = [pltpu.with_memory_space_constraint(a, held[id(s)]) if id(s) in held else a for a, s in args]
    return pl.pallas_call(
        kernel,
        name=name,
        in_specs=[spec for _, spec in args],
        out_specs=out_specs or [VMEM] * len(outs),
        out_shape=outs,
        scratch_shapes=list(scratch),
        input_output_aliases=aliases or {},
        compiler_params=pltpu.CompilerParams(vmem_limit_bytes=24 * 2**20),
        cost_estimate=pl.CostEstimate(flops=flops, bytes_accessed=moved, transcendentals=0),
    )(*arrays)


def on_device(x_in, w_reduce, w_spatial, w_expand, gain_mid, bias_mid, gain_out, bias_out):
    sections = lax.axis_size("section")
    strips = lax.axis_size("strip")
    section = lax.axis_index("section")
    strip = lax.axis_index("strip")
    core = lax.axis_index("col")
    tiles, c, rows, cols = x_in.shape
    cm = w_reduce.shape[1]
    half, wide = cm // 2, c // 2
    inner = rows - 2
    cells = tiles * rows * cols

    def swap(array):
        return lax.ppermute(array, "col", [(0, 1), (1, 0)])

    def from_section(array, level):
        total = None
        for step in range(1, sections - level):
            sent = lax.ppermute(array, "section", [(i, i + step) for i in range(sections - step)])
            total = sent if total is None else jnp.where(section - level == step, sent, total)
        return total

    def pairs(start):
        found = []
        for i in range(start, strips - 1, 2):
            found += [(i, i + 1), (i + 1, i)]
        return found

    (first,) = call(
        pack_first_kernel, "pack_first",
        [(a, HBM) for a in (w_reduce, gain_mid, bias_mid, gain_out, bias_out)],
        [near((half + 8, c))],
        [pltpu.VMEM((2, cm), F32)] * 2 + [pltpu.VMEM((1, c), F32)] * 2 + [pltpu.SemaphoreType.DMA((5,))],
        moved=4 * half * c,
    )
    first_sent = [from_section(first, level) for level in range(sections - 1)]
    (rest,) = call(
        pack_rest_kernel, "pack_rest", [(w_spatial, HBM), (w_expand, HBM)],
        [near((9 * half + wide, cm))], [pltpu.SemaphoreType.DMA((10,))], moved=4 * (9 * half + wide) * cm,
    )
    rest_sent = [from_section(rest, level) for level in range(sections - 1)]
    flat = x_in.reshape(tiles, c * rows, cols)
    (held,) = call(
        fetch_kernel, "fetch", [(flat, HBM)], [near(flat.shape)], [pltpu.SemaphoreType.DMA((tiles,))],
        moved=4 * cells * c,
    )
    rest_shapes = [near((9 * cm, 2 * cm), BF16), near((c, 3 * cm), BF16), near((c, 128))]
    own_reduce, own_spatial, own_expand, own_shift, own_terms = call(
        prepare_own_kernel, "prepare_own", [(w_reduce, FAR), (w_spatial, FAR), (w_expand, FAR), (first, VMEM)],
        [near((2 * cm, c), BF16)] + rest_shapes + [near((8, c))], moved=4 * cm * (2 * c + 9 * cm),
    )

    first_sent, held, _ = lax.optimization_barrier((first_sent, held, own_reduce))

    def reduce_weights(level):
        if level == sections - 1:
            return own_reduce, own_terms
        mine = first_sent[level]
        return call(
            functools.partial(prepare_reduce_kernel, level), "prepare_reduce",
            [(a, VMEM) for a in (mine, swap(mine), own_reduce, own_terms)],
            [near((2 * cm, c), BF16), near((8, c))], moved=4 * cm * c,
        )

    def rest_weights(level, terms):
        if level == sections - 1:
            return own_spatial, own_expand, own_shift
        mine = rest_sent[level]
        return call(
            functools.partial(prepare_rest_kernel, level), "prepare_rest",
            [(a, VMEM) for a in (mine, swap(mine), terms, own_spatial, own_expand, own_shift)],
            rest_shapes, moved=4 * cm * (c + 9 * cm),
        )

    def reduced_shapes(kind):
        count = 2 if kind == "border" else inner
        shapes = [near((tiles, count, cols, cm)), near((-(-tiles * count // 8) * 8, cm))]
        return shapes + ([near((tiles, cols, cm))] * 2 if kind == "border" else [])

    def reduce_call(kind, level, weights):
        return call(
            functools.partial(reduce_kernel, kind, rows), "reduce_" + kind,
            [(held, VMEM) if kind == "border" else (flat, HBM)] + [(a, VMEM) for a in weights],
            reduced_shapes(kind), [] if kind == "border" else tile_scratch, flops=3 * cells * c * cm, moved=4 * cells * c // 2,
        )

    tile_scratch = [pltpu.VMEM(flat.shape, F32), pltpu.SemaphoreType.DMA((tiles,))]

    def scratch(kind):
        count = 2 if kind == "border" else inner
        return [
            pltpu.VMEM((tiles, rows + 2, cols + 2 * PAD, cm), F32),
            pltpu.VMEM((tiles * count * cols, 9 * cm), BF16),
            pltpu.VMEM((tiles * count * cols, 9 * cm), BF16),
        ]

    def halos(msg_a, msg_b):
        halo_a = lax.ppermute(msg_a, "strip", pairs(0))
        halo_b = lax.ppermute(msg_b, "strip", pairs(1))
        at = jnp.where(core == 0, cols - 1, 0)
        edge_a = lax.dynamic_slice_in_dim(halo_a, at, 1, 1)
        edge_b = lax.dynamic_slice_in_dim(halo_b, at, 1, 1)
        return halo_a, halo_b, swap(jnp.concatenate([edge_a[:, 0], edge_b[:, 0]], axis=0))

    def block_call(kind, level, x, sent, weights, next_weights, before, halo=None):
        last = level == sections - 1
        (r_border, edge_border), (r_inner, edge_inner) = sent
        args = [(x, HBM if x is flat else VMEM)]
        args += [(a, VMEM) for a in (r_border, r_inner, edge_border, edge_inner)]
        if kind == "border":
            args += [(a, VMEM) for a in halo]
        args += [(a, VMEM) for a in weights]
        if not last:
            args += [(a, VMEM) for a in next_weights]
        args.append((before, VMEM if last and kind == "border" else ANY))
        count = 2 if kind == "border" else inner
        more, out_specs, aliases, held_out = scratch(kind), None, None, near((tiles, count, c, cols))
        if x is flat:
            more += tile_scratch
        if last:
            held_out = near(flat.shape)
        outs = [held_out] + ([] if last else reduced_shapes(kind))
        if last and kind == "border":
            outs = [pltpu.HBM(flat.shape, F32), held_out]
            out_specs = [ANY, VMEM]
            aliases = {len(args) - 1: 1}
            more.append(pltpu.SemaphoreType.DMA((tiles,)))
        return call(
            functools.partial(block_kernel, kind, rows, level, last), "block_" + kind, args, outs, more,
            flops=3 * cells * (13 if last else 17) * cm * cm, moved=4 * cells * c, out_specs=out_specs, aliases=aliases,
        )

    weights = reduce_weights(0)
    border = reduce_call("border", 0, weights)
    halo = halos(border[2], border[3])
    inside = reduce_call("inner", 0, weights)
    x_border = x_inner = flat
    for level in range(sections):
        last = level == sections - 1
        terms = weights[1]
        rest_of = tuple(rest_weights(level, terms)) + (terms,)
        sent = ((border[0], swap(border[1])), (inside[0], swap(inside[1])))
        if last:
            (part,) = block_call("inner", level, x_inner, sent, rest_of, None, first)
            whole = block_call("border", level, x_border, sent, rest_of, None, part, halo)[0]
        else:
            weights = reduce_weights(level + 1)
            x_border, *border = block_call("border", level, x_border, sent, rest_of, weights, first, halo)
            halo = halos(border[2], border[3])
            x_inner, *inside = block_call("inner", level, x_inner, sent, rest_of, weights, x_border)
    return whole.reshape(1, tiles, c, rows, cols)


def solution(mesh):
    in_specs = (
        P("groups", None, "strip", "col"),
        P("section", None, None),
        P("section", None, None, None),
        P("section", None, None),
        P("section", None, None),
        P("section", None, None),
        P("section", None),
        P("section", None),
    )
    out_specs = P("section", "groups", None, "strip", "col")
    return jax.shard_map(
        on_device, mesh=mesh, in_specs=in_specs, out_specs=out_specs, check_vma=False
    )
```

```python
import functools

import jax
import jax.numpy as jnp
from jax import lax
from jax.experimental import pallas as pl
from jax.experimental.pallas import tpu as pltpu
from jax.sharding import PartitionSpec as P

F32 = jnp.float32
BF16 = jnp.bfloat16
PAD = 8


def split(value):
    high = value.astype(BF16)
    return high, (value - high.astype(F32)).astype(BF16)


def dot(left, right):
    return jnp.dot(left, right, preferred_element_type=F32)


def dot_nt(left, right):
    return lax.dot_general(left, right, (((1,), (1,)), ((), ())), preferred_element_type=F32)


def first_core():
    return lax.axis_index("col") == 0


def even_strip():
    return lax.axis_index("strip") % 2 == 0


def column_of(row):
    return jnp.concatenate(
        [
            jnp.transpose(jnp.broadcast_to(row[:, at : at + 128], (128, 128)))
            for at in range(0, row.shape[1], 128)
        ],
        axis=0,
    )


def pack_first_kernel(
    w_reduce, gain_mid, bias_mid, gain_out, bias_out, first, gain_held, bias_held, gain_row, bias_row, sem
):
    half = w_reduce.shape[1] // 2
    cm = gain_mid.shape[2]
    low = pl.multiple_of(lax.axis_index("col") * half, half)
    moves = [
        (w_reduce.at[0, pl.ds(low, half), :], first.at[:half, :]),
        (gain_mid.at[0], gain_held),
        (bias_mid.at[0], bias_held),
        (gain_out, gain_row),
        (bias_out, bias_row),
    ]
    copies = [pltpu.make_async_copy(here, there, sem.at[i]) for i, (here, there) in enumerate(moves)]
    for copy in copies:
        copy.start()
    first[half : half + 8, :] = jnp.zeros((8, first.shape[1]), F32)
    for copy in copies:
        copy.wait()
    for i in range(2):
        first[half : half + 1, i * cm : (i + 1) * cm] = gain_held[i : i + 1, :]
        first[half : half + 1, (2 + i) * cm : (3 + i) * cm] = bias_held[i : i + 1, :]
    first[half + 1 : half + 2, :] = gain_row[...]
    first[half + 2 : half + 3, :] = bias_row[...]


def pack_rest_kernel(w_spatial, w_expand, before, rest, sem):
    half = w_spatial.shape[2] // 2
    wide = w_expand.shape[1] // 2
    low = pl.multiple_of(lax.axis_index("col") * half, half)
    at = pl.multiple_of(lax.axis_index("col") * wide, wide)
    moves = [(w_expand.at[0, pl.ds(at, wide), :], rest.at[9 * half :, :])]
    for tap in range(9):
        moves.append((w_spatial.at[0, tap, pl.ds(low, half), :], rest.at[tap * half : (tap + 1) * half, :]))
    copies = [pltpu.make_async_copy(here, there, sem.at[i]) for i, (here, there) in enumerate(moves)]
    for copy in copies:
        copy.start()
    for copy in copies:
        copy.wait()


def fetch_kernel(x, w_reduce, before, x_held, w_held, sem):
    copies = [pltpu.make_async_copy(x.at[t], x_held.at[t], sem.at[t]) for t in range(x.shape[0])]
    copies.append(pltpu.make_async_copy(w_reduce.at[0], w_held, sem.at[x.shape[0]]))
    for copy in copies:
        copy.start()
    for copy in copies:
        copy.wait()


def corner_kernel(halo_a, halo_b, *refs):
    out = refs[-1]
    first = first_core()
    tiles, cols = halo_a.shape[:2]
    for i, halo in enumerate((halo_a, halo_b)):
        for tile in range(tiles):
            side = jnp.where(first, halo[tile, cols - 1 : cols, :], halo[tile, 0:1, :])
            out[i * tiles + tile : i * tiles + tile + 1, :] = side


def store_reduce(w_high, at, rows):
    cm = w_high.shape[0] // 2
    high, low = split(rows)
    w_high[at : at + rows.shape[0], :] = high
    w_high[cm + at : cm + at + rows.shape[0], :] = low


def store_rest(tap_rows, expand_rows, gain_out, w_spatial, w_expand):
    cm = w_expand.shape[1] // 3
    for tap in range(9):
        high, low = split(jnp.transpose(tap_rows(tap)))
        w_spatial[tap * cm : (tap + 1) * cm, :cm] = high
        w_spatial[tap * cm : (tap + 1) * cm, cm:] = low
    high, low = split(expand_rows * column_of(gain_out))
    w_expand[:, :cm] = high
    w_expand[:, cm : 2 * cm] = low
    w_expand[:, 2 * cm :] = high


def prepare_own_kernel(w_reduce, w_spatial, w_expand, first, before, out_reduce, out_spatial, out_expand, out_shift, out_terms):
    half = w_reduce.shape[0] // 2
    store_reduce(out_reduce, 0, w_reduce[...])
    terms = first[half : half + 8, :]
    out_terms[...] = terms
    out_shift[...] = column_of(terms[2:3, :])
    store_rest(lambda tap: w_spatial[0, tap], w_expand[0], terms[1:2, :], out_spatial, out_expand)


def prepare_reduce_kernel(level, mine, other, w_reduce, first, out_reduce, out_terms):
    half = mine.shape[0] - 8

    @pl.when(lax.axis_index("section") == level)
    def _():
        store_reduce(out_reduce, 0, w_reduce[...])
        out_terms[...] = first[half:, :]

    @pl.when(lax.axis_index("section") != level)
    def _():
        out_terms[...] = mine[half:, :]
        for core in range(2):

            @pl.when(lax.axis_index("col") == core)
            def _(core=core):
                store_reduce(out_reduce, core * half, mine[:half, :])
                store_reduce(out_reduce, (1 - core) * half, other[:half, :])


def prepare_rest_kernel(
    level, mine, other, terms, own_spatial, own_expand, own_shift, out_spatial, out_expand, out_shift
):
    cm = own_expand.shape[1] // 3
    half, wide = cm // 2, own_expand.shape[0] // 2

    @pl.when(lax.axis_index("section") == level)
    def _():
        out_spatial[...] = own_spatial[...]
        out_expand[...] = own_expand[...]
        out_shift[...] = own_shift[...]

    @pl.when(lax.axis_index("section") != level)
    def _():
        out_shift[...] = column_of(terms[2:3, :])
        for core in range(2):

            @pl.when(lax.axis_index("col") == core)
            def _(core=core):
                low, up = (mine, other) if core == 0 else (other, mine)

                def tap_rows(tap):
                    at = slice(tap * half, (tap + 1) * half)
                    return jnp.concatenate([low[at, :], up[at, :]], axis=0)

                expand = jnp.concatenate([low[9 * half :, :], up[9 * half :, :]], axis=0)
                store_rest(tap_rows, expand, terms[1:2, :], out_spatial, out_expand)


def members(kind, rows):
    return (0, rows - 1) if kind == "border" else tuple(range(1, rows - 1))


def reduce_step(tile, field, w_reduce, terms, r_out, edge, msgs):
    cm = w_reduce.shape[0] // 2
    count, cols = r_out.shape[1:3]
    high, low = split(field)
    both = dot(w_reduce[...], high)
    total = both[:cm] + both[cm:] + dot(w_reduce[:cm, :], low)
    gain, shift = terms[0:1, 0:cm], terms[0:1, 2 * cm : 3 * cm]
    even, first = even_strip(), first_core()
    turned = []
    for j in range(count):
        part = jnp.maximum(jnp.transpose(total[:, j * cols : (j + 1) * cols]) * gain + shift, 0.0)
        r_out[tile, j] = part
        at = tile * count + j
        edge[at : at + 1, :] = jnp.where(first, part[cols - 1 : cols, :], part[0:1, :])
        turned.append(part)
    if msgs:
        msgs[0][tile] = jnp.where(even, turned[-1], turned[0])
        msgs[1][tile] = jnp.where(even, turned[0], turned[-1])


def field_rows(x, kind, rows, tile, j):
    if len(x.shape) == 3:
        return x[tile, pl.ds(members(kind, rows)[j], x.shape[1] // rows, stride=rows), :]
    return x[tile, j]


def reduce_kernel(kind, rows, x, w_reduce, terms, before, r_out, edge, *msgs):
    edge[...] = jnp.zeros_like(edge)
    count = r_out.shape[1]
    for tile in range(x.shape[0]):
        field = jnp.concatenate([field_rows(x, kind, rows, tile, j) for j in range(count)], axis=1)
        reduce_step(tile, field, w_reduce, terms, r_out, edge, msgs)


def block_kernel(kind, rows, level, last, *refs):
    refs = list(refs)

    def take(n):
        taken, refs[:n] = refs[:n], []
        return taken

    border = kind == "border"
    x, r_border, r_inner, edge_border, edge_inner = take(5)
    if border:
        halo_a, halo_b, corners = take(3)
    w_spatial, w_expand, shift_out, terms = take(4)
    if not last:
        next_reduce, next_terms = take(2)
    if last and border:
        take(1)
    else:
        take(1)
    outs = take(2 if last and border else 1)
    if not last:
        r_out, edge_out = take(2)
        msgs = take(2) if border else []
        edge_out[...] = jnp.zeros_like(edge_out)
    padded, taps_high, taps_low = take(3)
    tiles, _, cols, cm = r_border.shape
    chosen = members(kind, rows)
    count = len(chosen)
    inner = members("inner", rows)
    even, first = even_strip(), first_core()
    gain, shift = terms[0:1, cm : 2 * cm], terms[0:1, 3 * cm : 4 * cm]
    keep = lax.axis_index("section") >= level

    def row_and_side(tile, i):
        if i in (-1, rows):
            from_a = even if i == rows else jnp.logical_not(even)
            side_a, side_b = corners[tile : tile + 1, :], corners[tiles + tile : tiles + tile + 1, :]
            return jnp.where(from_a, halo_a[tile], halo_b[tile]), jnp.where(from_a, side_a, side_b)
        if i in (0, rows - 1):
            j = 0 if i == 0 else 1
            return r_border[tile, j], edge_border[2 * tile + j : 2 * tile + j + 1, :]
        j = inner.index(i)
        at = tile * len(inner) + j
        return r_inner[tile, j], edge_inner[at : at + 1, :]

    span = count * cols
    group = 2 if last and border and tiles % 2 == 0 else tiles
    for g in range(0, tiles, group):
        for tile in range(g, g + group):
            for i in sorted({r + p for r in chosen for p in (-1, 0, 1)}):
                field, side = row_and_side(tile, i)
                slot = padded.at[tile, i + 1]
                slot[PAD : PAD + cols, :] = field
                slot[PAD - 1 : PAD, :] = jnp.where(first, 0.0, side)
                slot[PAD + cols : PAD + cols + 1, :] = jnp.where(first, side, 0.0)
                for q in range(3):
                    high, low = split(field if q == 1 else slot[PAD - 1 + q : PAD - 1 + q + cols, :])
                    for j, r in enumerate(chosen):
                        p = i - r + 1
                        if 0 <= p <= 2:
                            lanes = slice((3 * p + q) * cm, (3 * p + q + 1) * cm)
                            at = (tile * count + j) * cols
                            taps_high[at : at + cols, lanes] = high
                            taps_low[at : at + cols, lanes] = low
        at = slice(g * span, (g + group) * span)
        both = dot(taps_high[at, :], w_spatial[...])
        spatial = both[:, :cm] + both[:, cm:] + dot(taps_low[at, :], w_spatial[:, :cm])
        high, low = split(jnp.maximum(spatial * gain + shift, 0.0))
        middle = jnp.concatenate([high, high, low], axis=1)
        for tile in range(g, g + group):
            k = tile - g
            branch = dot_nt(w_expand[...], middle[k * span : (k + 1) * span])
            after = []
            for j in range(count):
                before = field_rows(x, kind, rows, tile, j)
                new = jnp.maximum(before + branch[:, j * cols : (j + 1) * cols] + shift_out[...], 0.0)
                after.append(jnp.where(keep, new, before))
                if last:
                    whole = outs[-1]
                    whole[tile, pl.ds(chosen[j], whole.shape[1] // rows, stride=rows), :] = after[j]
                else:
                    outs[0][tile, j] = after[j]
            if not last:
                field = jnp.concatenate(after, axis=1)
                reduce_step(tile, field, next_reduce, next_terms, r_out, edge_out, msgs)
            if last and border:
                sem = refs[0]
                pltpu.make_async_copy(outs[1].at[tile], outs[0].at[tile], sem.at[tile]).start()
    if last and border:
        sem = refs[0]
        for tile in range(tiles):
            pltpu.make_async_copy(outs[1].at[tile], outs[0].at[tile], sem.at[tile]).wait()


VMEM = pl.BlockSpec(memory_space=pltpu.VMEM)
ANY = pl.BlockSpec(memory_space=pl.ANY)
HBM = pl.BlockSpec(memory_space=pl.ANY)
FAR = pl.BlockSpec(memory_space=pltpu.VMEM)


def near(shape, dtype=F32):
    return pltpu.VMEM(shape, dtype)


def call(kernel, name, args, outs, scratch=(), flops=0, moved=0, specs=None, out_specs=None, aliases=None):
    held = {id(VMEM): pltpu.VMEM, id(HBM): pltpu.HBM, id(FAR): pltpu.HBM}
    arrays = [pltpu.with_memory_space_constraint(a, held[id(s)]) if id(s) in held else a for a, s in args]
    return pl.pallas_call(
        kernel,
        name=name,
        in_specs=[spec for _, spec in args],
        out_specs=out_specs or [VMEM] * len(outs),
        out_shape=outs,
        scratch_shapes=list(scratch),
        input_output_aliases=aliases or {},
        compiler_params=pltpu.CompilerParams(vmem_limit_bytes=16 * 2**20),
        cost_estimate=pl.CostEstimate(flops=flops, bytes_accessed=moved, transcendentals=0),
    )(*arrays)


def on_device(x_in, w_reduce, w_spatial, w_expand, gain_mid, bias_mid, gain_out, bias_out):
    sections = lax.axis_size("section")
    strips = lax.axis_size("strip")
    section = lax.axis_index("section")
    tiles, c, rows, cols = x_in.shape
    cm = w_reduce.shape[1]
    half, wide = cm // 2, c // 2
    inner = rows - 2
    cells = tiles * rows * cols

    def swap(array):
        return lax.ppermute(array, "col", [(0, 1), (1, 0)])

    def from_section(array, level):
        total = None
        for step in range(1, sections - level):
            sent = lax.ppermute(array, "section", [(i, i + step) for i in range(sections - step)])
            total = sent if total is None else jnp.where(section - level == step, sent, total)
        return total

    def pairs(start, level):
        found = []
        for i in range(start, strips - 1, 2):
            for j in range(level, sections):
                above, below = i * sections + j, (i + 1) * sections + j
                found += [(above, below), (below, above)]
        return found

    (first,) = call(
        pack_first_kernel, "pack_first", [(a, HBM) for a in (w_reduce, gain_mid, bias_mid, gain_out, bias_out)],
        [near((half + 8, c))],
        [pltpu.VMEM((2, cm), F32)] * 2 + [pltpu.VMEM((1, c), F32)] * 2 + [pltpu.SemaphoreType.DMA((5,))],
        moved=4 * half * c,
    )
    first_sent = [from_section(first, level) for level in range(sections - 1)]
    flat = x_in.reshape(tiles, c * rows, cols)
    held, w_held = call(
        fetch_kernel, "fetch", [(flat, HBM), (w_reduce, HBM), (first, ANY)], [near(flat.shape), near((cm, c))],
        [pltpu.SemaphoreType.DMA((tiles + 1,))], moved=4 * cells * c,
    )
    (rest,) = call(
        pack_rest_kernel, "pack_rest", [(w_spatial, HBM), (w_expand, HBM), (w_held, ANY)],
        [near((9 * half + wide, cm))], [pltpu.SemaphoreType.DMA((10,))], moved=4 * (9 * half + wide) * cm,
    )
    rest_sent = [from_section(rest, level) for level in range(sections - 1)]
    rest_shapes = [near((9 * cm, 2 * cm), BF16), near((c, 3 * cm), BF16), near((c, 128))]
    first_sent, held, w_held, _ = lax.optimization_barrier((first_sent, held, w_held, rest))

    def prepare_own(before):
        return call(
            prepare_own_kernel, "prepare_own",
            [(w_held, VMEM), (w_spatial, FAR), (w_expand, FAR), (first, VMEM), (before, ANY)],
            [near((2 * cm, c), BF16)] + rest_shapes + [near((8, c))], moved=4 * cm * (2 * c + 9 * cm),
        )

    def reduce_weights(level):
        if level == sections - 1 and level > 0:
            return own[0], own[4]
        if sections == 1:
            return prepare_own(first)[::4]
        mine = first_sent[level]
        return call(
            functools.partial(prepare_reduce_kernel, level), "prepare_reduce",
            [(a, VMEM) for a in (mine, swap(mine), w_held, first)],
            [near((2 * cm, c), BF16), near((8, c))], moved=4 * cm * c,
        )

    def rest_weights(level, terms):
        if level == sections - 1:
            return own[1:4]
        mine, _ = lax.optimization_barrier((rest_sent[level], halo[3]))
        return call(
            functools.partial(prepare_rest_kernel, level), "prepare_rest",
            [(a, VMEM) for a in (mine, swap(mine), terms, *own[1:4])],
            rest_shapes, moved=4 * cm * (c + 9 * cm),
        )

    def reduced_shapes(kind):
        count = 2 if kind == "border" else inner
        shapes = [near((tiles, count, cols, cm)), near((-(-tiles * count // 8) * 8, cm))]
        return shapes + ([near((tiles, cols, cm))] * 2 if kind == "border" else [])

    def reduce_call(kind, level, weights, before):
        return call(
            functools.partial(reduce_kernel, kind, rows), "reduce_" + kind,
            [(held, VMEM)] + [(a, VMEM) for a in weights] + [(before, ANY)],
            reduced_shapes(kind), flops=3 * cells * c * cm, moved=4 * cells * c // 2,
        )

    def scratch(kind):
        count = 2 if kind == "border" else inner
        return [
            pltpu.VMEM((tiles, rows + 2, cols + 2 * PAD, cm), F32),
            pltpu.VMEM((tiles * count * cols, 9 * cm), BF16),
            pltpu.VMEM((tiles * count * cols, 9 * cm), BF16),
        ]

    def halos(msg_a, msg_b, swapped, level):
        axes = ("strip", "section")
        msg_a, _ = lax.optimization_barrier((msg_a, swapped))
        return lax.ppermute(msg_a, axes, pairs(0, level)), lax.ppermute(msg_b, axes, pairs(1, level))

    def with_corners(halo, before):
        args = [(a, VMEM) for a in halo] + [(a, ANY) for a in before]
        (corners,) = call(corner_kernel, "corners", args, [near((2 * tiles, cm))])
        return halo + (swap(corners), corners)

    def block_call(kind, level, x, sent, weights, next_weights, before, halo=None):
        last = level == sections - 1
        (r_border, edge_border), (r_inner, edge_inner) = sent
        args = [(x, VMEM)]
        args += [(a, VMEM) for a in (r_border, r_inner, edge_border, edge_inner)]
        if kind == "border":
            args += [(a, VMEM) for a in halo[:3]]
        args += [(a, VMEM) for a in weights]
        if not last:
            args += [(a, VMEM) for a in next_weights]
        args.append((before, VMEM if last and kind == "border" else ANY))
        count = 2 if kind == "border" else inner
        more, out_specs, aliases, held_out = scratch(kind), None, None, near((tiles, count, c, cols))
        if last:
            held_out = near(flat.shape)
        outs = [held_out] + ([] if last else reduced_shapes(kind))
        if last and kind == "border":
            outs = [pltpu.HBM(flat.shape, F32), held_out]
            out_specs = [ANY, VMEM]
            aliases = {len(args) - 1: 1}
            more.append(pltpu.SemaphoreType.DMA((tiles,)))
        return call(
            functools.partial(block_kernel, kind, rows, level, last), "block_" + kind, args, outs, more,
            flops=3 * cells * (13 if last else 17) * cm * cm, moved=4 * cells * c, out_specs=out_specs, aliases=aliases,
        )

    weights = reduce_weights(0)
    border = reduce_call("border", 0, weights, first)
    edges = swap(border[1])
    halo = halos(border[2], border[3], edges, 0)
    own = prepare_own(border[1])
    inside = reduce_call("inner", 0, weights, border[1])
    sent = ((border[0], edges), (inside[0], swap(inside[1])))
    halo = with_corners(halo, (own[4], sent[0][1], sent[1][1]))
    x_border = x_inner = held
    for level in range(sections):
        last = level == sections - 1
        terms = weights[1]
        rest_of = tuple(rest_weights(level, terms)) + (terms,)
        if level > 0:
            sent = ((border[0], edges), (inside[0], swap(inside[1])))
        if last:
            (part,) = block_call("inner", level, x_inner, sent, rest_of, None, first)
            if level > 0:
                halo = with_corners(halo, (part,))
            whole = block_call("border", level, x_border, sent, rest_of, None, part, halo)[0]
        else:
            weights = reduce_weights(level + 1)
            x_border, *border = block_call("border", level, x_border, sent, rest_of, weights, first, halo)
            edges = swap(border[1])
            halo = halos(border[2], border[3], edges, level + 1)
            x_inner, *inside = block_call("inner", level, x_inner, sent, rest_of, weights, x_border)
            if level + 1 < sections - 1:
                halo = with_corners(halo, (inside[1],))
    return whole.reshape(1, tiles, c, rows, cols)


def solution(mesh):
    in_specs = (
        P("groups", None, "strip", "col"),
        P("section", None, None),
        P("section", None, None, None),
        P("section", None, None),
        P("section", None, None),
        P("section", None, None),
        P("section", None),
        P("section", None),
    )
    out_specs = P("section", "groups", None, "strip", "col")
    return jax.shard_map(
        on_device, mesh=mesh, in_specs=in_specs, out_specs=out_specs, check_vma=False
    )
```

```python
import functools

import jax
import jax.numpy as jnp
from jax import lax
from jax.experimental import pallas as pl
from jax.experimental.pallas import tpu as pltpu
from jax.sharding import PartitionSpec as P

F32 = jnp.float32
BF16 = jnp.bfloat16
PAD = 8


def split(value):
    high = value.astype(BF16)
    return high, (value - high.astype(F32)).astype(BF16)


def dot(left, right):
    return jnp.dot(left, right, preferred_element_type=F32)


def dot_nt(left, right):
    return lax.dot_general(left, right, (((1,), (1,)), ((), ())), preferred_element_type=F32)


def first_core():
    return lax.axis_index("col") == 0


def even_strip():
    return lax.axis_index("strip") % 2 == 0


def column_of(row):
    return jnp.concatenate(
        [
            jnp.transpose(jnp.broadcast_to(row[:, at : at + 128], (128, 128)))
            for at in range(0, row.shape[1], 128)
        ],
        axis=0,
    )


def pack_first_kernel(
    w_reduce, gain_mid, bias_mid, gain_out, bias_out, first, gain_held, bias_held, gain_row, bias_row, sem
):
    half = w_reduce.shape[1] // 2
    cm = gain_mid.shape[2]
    low = pl.multiple_of(lax.axis_index("col") * half, half)
    moves = [
        (w_reduce.at[0, pl.ds(low, half), :], first.at[:half, :]),
        (gain_mid.at[0], gain_held),
        (bias_mid.at[0], bias_held),
        (gain_out, gain_row),
        (bias_out, bias_row),
    ]
    copies = [pltpu.make_async_copy(here, there, sem.at[i]) for i, (here, there) in enumerate(moves)]
    for copy in copies:
        copy.start()
    first[half : half + 8, :] = jnp.zeros((8, first.shape[1]), F32)
    for copy in copies:
        copy.wait()
    for i in range(2):
        first[half : half + 1, i * cm : (i + 1) * cm] = gain_held[i : i + 1, :]
        first[half : half + 1, (2 + i) * cm : (3 + i) * cm] = bias_held[i : i + 1, :]
    first[half + 1 : half + 2, :] = gain_row[...]
    first[half + 2 : half + 3, :] = bias_row[...]


def pack_rest_kernel(w_spatial, w_expand, before, rest, sem):
    half = w_spatial.shape[2] // 2
    wide = w_expand.shape[1] // 2
    low = pl.multiple_of(lax.axis_index("col") * half, half)
    at = pl.multiple_of(lax.axis_index("col") * wide, wide)
    moves = [(w_expand.at[0, pl.ds(at, wide), :], rest.at[9 * half :, :])]
    for tap in range(9):
        moves.append((w_spatial.at[0, tap, pl.ds(low, half), :], rest.at[tap * half : (tap + 1) * half, :]))
    copies = [pltpu.make_async_copy(here, there, sem.at[i]) for i, (here, there) in enumerate(moves)]
    for copy in copies:
        copy.start()
    for copy in copies:
        copy.wait()


def fetch_kernel(x, w_reduce, before, x_held, w_held, sem):
    copies = [pltpu.make_async_copy(x.at[t], x_held.at[t], sem.at[t]) for t in range(x.shape[0])]
    copies.append(pltpu.make_async_copy(w_reduce.at[0], w_held, sem.at[x.shape[0]]))
    for copy in copies:
        copy.start()
    for copy in copies:
        copy.wait()


def corner_kernel(count, *refs):
    out = refs[-1]
    first = first_core()
    tiles = refs[0].shape[0]
    cols = refs[0].shape[1]
    out[...] = jnp.zeros_like(out)
    for i in range(count):
        for tile in range(tiles):
            side = jnp.where(first, refs[i][tile, cols - 1 : cols, :], refs[i][tile, 0:1, :])
            out[i * tiles + tile : i * tiles + tile + 1, :] = side


def append_kernel(msg, edges, out):
    even = even_strip()
    tiles = msg.shape[0]
    at = msg.shape[1] - 8
    for tile in range(tiles):
        out[tile, at : at + 1, :] = jnp.where(
            even, edges[2 * tile + 1 : 2 * tile + 2, :], edges[2 * tile : 2 * tile + 1, :]
        )


def store_reduce(w_high, at, rows):
    cm = w_high.shape[0] // 2
    high, low = split(rows)
    w_high[at : at + rows.shape[0], :] = high
    w_high[cm + at : cm + at + rows.shape[0], :] = low


def store_rest(tap_rows, expand_rows, gain_out, w_spatial, w_expand):
    cm = w_expand.shape[1] // 3
    for tap in range(9):
        high, low = split(jnp.transpose(tap_rows(tap)))
        w_spatial[tap * cm : (tap + 1) * cm, :cm] = high
        w_spatial[tap * cm : (tap + 1) * cm, cm:] = low
    high, low = split(expand_rows * column_of(gain_out))
    w_expand[:, :cm] = high
    w_expand[:, cm : 2 * cm] = low
    w_expand[:, 2 * cm :] = high


def prepare_own_kernel(w_reduce, w_spatial, w_expand, first, before, out_reduce, out_spatial, out_expand, out_shift, out_terms):
    half = w_reduce.shape[0] // 2
    store_reduce(out_reduce, 0, w_reduce[...])
    terms = first[half : half + 8, :]
    out_terms[...] = terms
    out_shift[...] = column_of(terms[2:3, :])
    store_rest(lambda tap: w_spatial[0, tap], w_expand[0], terms[1:2, :], out_spatial, out_expand)


def prepare_reduce_kernel(level, mine, other, w_reduce, first, out_reduce, out_terms):
    half = mine.shape[0] - 8

    @pl.when(lax.axis_index("section") == level)
    def _():
        store_reduce(out_reduce, 0, w_reduce[...])
        out_terms[...] = first[half:, :]

    @pl.when(lax.axis_index("section") != level)
    def _():
        out_terms[...] = mine[half:, :]
        for core in range(2):

            @pl.when(lax.axis_index("col") == core)
            def _(core=core):
                store_reduce(out_reduce, core * half, mine[:half, :])
                store_reduce(out_reduce, (1 - core) * half, other[:half, :])


def prepare_rest_kernel(
    level, mine, other, terms, own_spatial, own_expand, own_shift, out_spatial, out_expand, out_shift
):
    cm = own_expand.shape[1] // 3
    half, wide = cm // 2, own_expand.shape[0] // 2

    @pl.when(lax.axis_index("section") == level)
    def _():
        out_spatial[...] = own_spatial[...]
        out_expand[...] = own_expand[...]
        out_shift[...] = own_shift[...]

    @pl.when(lax.axis_index("section") != level)
    def _():
        out_shift[...] = column_of(terms[2:3, :])
        for core in range(2):

            @pl.when(lax.axis_index("col") == core)
            def _(core=core):
                low, up = (mine, other) if core == 0 else (other, mine)

                def tap_rows(tap):
                    at = slice(tap * half, (tap + 1) * half)
                    return jnp.concatenate([low[at, :], up[at, :]], axis=0)

                expand = jnp.concatenate([low[9 * half :, :], up[9 * half :, :]], axis=0)
                store_rest(tap_rows, expand, terms[1:2, :], out_spatial, out_expand)


def members(kind, rows):
    return (0, rows - 1) if kind == "border" else tuple(range(1, rows - 1))


def reduce_step(tile, field, w_reduce, terms, r_out, edge, msgs):
    cm = w_reduce.shape[0] // 2
    count, cols = r_out.shape[1:3]
    high, low = split(field)
    both = dot(w_reduce[...], high)
    total = both[:cm] + both[cm:] + dot(w_reduce[:cm, :], low)
    gain, shift = terms[0:1, 0:cm], terms[0:1, 2 * cm : 3 * cm]
    even, first = even_strip(), first_core()
    turned = []
    for j in range(count):
        part = jnp.maximum(jnp.transpose(total[:, j * cols : (j + 1) * cols]) * gain + shift, 0.0)
        r_out[tile, j] = part
        at = tile * count + j
        edge[at : at + 1, :] = jnp.where(first, part[cols - 1 : cols, :], part[0:1, :])
        turned.append(part)
    if msgs:
        msgs[0][tile, :cols, :] = jnp.where(even, turned[-1], turned[0])
        if msgs[0].shape[1] > cols:
            msgs[0][tile, cols:, :] = jnp.zeros((msgs[0].shape[1] - cols, cm), F32)
        msgs[1][tile] = jnp.where(even, turned[0], turned[-1])


def field_rows(x, kind, rows, tile, j):
    if len(x.shape) == 3:
        return x[tile, pl.ds(members(kind, rows)[j], x.shape[1] // rows, stride=rows), :]
    return x[tile, j]


def reduce_kernel(kind, rows, x, w_reduce, terms, before, r_out, edge, *msgs):
    edge[...] = jnp.zeros_like(edge)
    count = r_out.shape[1]
    for tile in range(x.shape[0]):
        field = jnp.concatenate([field_rows(x, kind, rows, tile, j) for j in range(count)], axis=1)
        reduce_step(tile, field, w_reduce, terms, r_out, edge, msgs)


def block_kernel(kind, rows, level, last, *refs):
    refs = list(refs)

    def take(n):
        taken, refs[:n] = refs[:n], []
        return taken

    border = kind == "border"
    x, r_border, r_inner, edge_border, edge_inner = take(5)
    if border:
        halo_a, halo_b, corners = take(3)
    w_spatial, w_expand, shift_out, terms = take(4)
    if not last:
        next_reduce, next_terms = take(2)
    if last and border:
        take(1)
    else:
        take(1)
    outs = take(2 if last and border else 1)
    if not last:
        r_out, edge_out = take(2)
        msgs = take(2) if border else []
        edge_out[...] = jnp.zeros_like(edge_out)
    padded, taps_high, taps_low = take(3)
    tiles, _, cols, cm = r_border.shape
    chosen = members(kind, rows)
    count = len(chosen)
    inner = members("inner", rows)
    even, first = even_strip(), first_core()
    gain, shift = terms[0:1, cm : 2 * cm], terms[0:1, 3 * cm : 4 * cm]
    keep = lax.axis_index("section") >= level

    def row_and_side(tile, i):
        if i in (-1, rows):
            from_a = even if i == rows else jnp.logical_not(even)
            side_b = corners[tile : tile + 1, :]
            side_a = halo_a[tile, cols : cols + 1, :] if level else corners[tiles + tile : tiles + tile + 1, :]
            return jnp.where(from_a, halo_a[tile, :cols, :], halo_b[tile]), jnp.where(from_a, side_a, side_b)
        if i in (0, rows - 1):
            j = 0 if i == 0 else 1
            return r_border[tile, j], edge_border[2 * tile + j : 2 * tile + j + 1, :]
        j = inner.index(i)
        at = tile * len(inner) + j
        return r_inner[tile, j], edge_inner[at : at + 1, :]

    span = count * cols
    group = 2 if last and border and tiles % 2 == 0 else tiles
    for g in range(0, tiles, group):
        for tile in range(g, g + group):
            for i in sorted({r + p for r in chosen for p in (-1, 0, 1)}):
                field, side = row_and_side(tile, i)
                slot = padded.at[tile, i + 1]
                slot[PAD : PAD + cols, :] = field
                slot[PAD - 1 : PAD, :] = jnp.where(first, 0.0, side)
                slot[PAD + cols : PAD + cols + 1, :] = jnp.where(first, side, 0.0)
                for q in range(3):
                    high, low = split(field if q == 1 else slot[PAD - 1 + q : PAD - 1 + q + cols, :])
                    for j, r in enumerate(chosen):
                        p = i - r + 1
                        if 0 <= p <= 2:
                            lanes = slice((3 * p + q) * cm, (3 * p + q + 1) * cm)
                            at = (tile * count + j) * cols
                            taps_high[at : at + cols, lanes] = high
                            taps_low[at : at + cols, lanes] = low
        at = slice(g * span, (g + group) * span)
        both = dot(taps_high[at, :], w_spatial[...])
        spatial = both[:, :cm] + both[:, cm:] + dot(taps_low[at, :], w_spatial[:, :cm])
        high, low = split(jnp.maximum(spatial * gain + shift, 0.0))
        middle = jnp.concatenate([high, high, low], axis=1)
        for tile in range(g, g + group):
            k = tile - g
            branch = dot_nt(w_expand[...], middle[k * span : (k + 1) * span])
            after = []
            for j in range(count):
                before = field_rows(x, kind, rows, tile, j)
                new = jnp.maximum(before + branch[:, j * cols : (j + 1) * cols] + shift_out[...], 0.0)
                after.append(jnp.where(keep, new, before) if level else new)
                if last:
                    whole = outs[-1]
                    whole[tile, pl.ds(chosen[j], whole.shape[1] // rows, stride=rows), :] = after[j]
                else:
                    outs[0][tile, j] = after[j]
            if not last:
                field = jnp.concatenate(after, axis=1)
                reduce_step(tile, field, next_reduce, next_terms, r_out, edge_out, msgs)
            if last and border:
                sem = refs[0]
                pltpu.make_async_copy(outs[1].at[tile], outs[0].at[tile], sem.at[tile]).start()
    if last and border:
        sem = refs[0]
        for tile in range(tiles):
            pltpu.make_async_copy(outs[1].at[tile], outs[0].at[tile], sem.at[tile]).wait()


VMEM = pl.BlockSpec(memory_space=pltpu.VMEM)
ANY = pl.BlockSpec(memory_space=pl.ANY)
HBM = pl.BlockSpec(memory_space=pl.ANY)
FAR = pl.BlockSpec(memory_space=pltpu.VMEM)


def near(shape, dtype=F32):
    return pltpu.VMEM(shape, dtype)


def call(kernel, name, args, outs, scratch=(), flops=0, moved=0, specs=None, out_specs=None, aliases=None):
    held = {id(VMEM): pltpu.VMEM, id(HBM): pltpu.HBM, id(FAR): pltpu.HBM}
    arrays = [pltpu.with_memory_space_constraint(a, held[id(s)]) if id(s) in held else a for a, s in args]
    return pl.pallas_call(
        kernel,
        name=name,
        in_specs=[spec for _, spec in args],
        out_specs=out_specs or [VMEM] * len(outs),
        out_shape=outs,
        scratch_shapes=list(scratch),
        input_output_aliases=aliases or {},
        compiler_params=pltpu.CompilerParams(vmem_limit_bytes=16 * 2**20),
        cost_estimate=pl.CostEstimate(flops=flops, bytes_accessed=moved, transcendentals=0),
    )(*arrays)


def on_device(x_in, w_reduce, w_spatial, w_expand, gain_mid, bias_mid, gain_out, bias_out):
    sections = lax.axis_size("section")
    strips = lax.axis_size("strip")
    section = lax.axis_index("section")
    tiles, c, rows, cols = x_in.shape
    cm = w_reduce.shape[1]
    half, wide = cm // 2, c // 2
    inner = rows - 2
    cells = tiles * rows * cols

    def swap(array):
        return lax.ppermute(array, "col", [(0, 1), (1, 0)])

    def from_section(array, level):
        total = None
        for step in range(1, sections - level):
            sent = lax.ppermute(array, "section", [(i, i + step) for i in range(sections - step)])
            total = sent if total is None else jnp.where(section - level == step, sent, total)
        return total

    def pairs(start, level):
        found = []
        for i in range(start, strips - 1, 2):
            for j in range(level, sections):
                above, below = i * sections + j, (i + 1) * sections + j
                found += [(above, below), (below, above)]
        return found

    (first,) = call(
        pack_first_kernel, "pack_first", [(a, HBM) for a in (w_reduce, gain_mid, bias_mid, gain_out, bias_out)],
        [near((half + 8, c))],
        [pltpu.VMEM((2, cm), F32)] * 2 + [pltpu.VMEM((1, c), F32)] * 2 + [pltpu.SemaphoreType.DMA((5,))],
        moved=4 * half * c,
    )
    first_sent = [from_section(first, level) for level in range(sections - 1)]
    flat = x_in.reshape(tiles, c * rows, cols)
    held, w_held = call(
        fetch_kernel, "fetch", [(flat, HBM), (w_reduce, HBM), (first, ANY)], [near(flat.shape), near((cm, c))],
        [pltpu.SemaphoreType.DMA((tiles + 1,))], moved=4 * cells * c,
    )
    (rest,) = call(
        pack_rest_kernel, "pack_rest", [(w_spatial, HBM), (w_expand, HBM), (w_held, ANY)],
        [near((9 * half + wide, cm))], [pltpu.SemaphoreType.DMA((10,))], moved=4 * (9 * half + wide) * cm,
    )
    rest_sent = [from_section(rest, level) for level in range(sections - 1)]
    rest_shapes = [near((9 * cm, 2 * cm), BF16), near((c, 3 * cm), BF16), near((c, 128))]
    first_sent, held, w_held, _ = lax.optimization_barrier((first_sent, held, w_held, rest))

    def prepare_own(before):
        return call(
            prepare_own_kernel, "prepare_own",
            [(w_held, VMEM), (w_spatial, FAR), (w_expand, FAR), (first, VMEM), (before, ANY)],
            [near((2 * cm, c), BF16)] + rest_shapes + [near((8, c))], moved=4 * cm * (2 * c + 9 * cm),
        )

    def reduce_weights(level):
        if level == sections - 1 and level > 0:
            return own[0], own[4]
        if sections == 1:
            return prepare_own(first)[::4]
        mine = first_sent[level]
        return call(
            functools.partial(prepare_reduce_kernel, level), "prepare_reduce",
            [(a, VMEM) for a in (mine, swap(mine), w_held, first)],
            [near((2 * cm, c), BF16), near((8, c))], moved=4 * cm * c,
        )

    def rest_weights(level, terms):
        if level == sections - 1:
            return own[1:4]
        mine, _ = lax.optimization_barrier((rest_sent[level], halo[3]))
        return call(
            functools.partial(prepare_rest_kernel, level), "prepare_rest",
            [(a, VMEM) for a in (mine, swap(mine), terms, *own[1:4])],
            rest_shapes, moved=4 * cm * (c + 9 * cm),
        )

    def reduced_shapes(kind, level):
        room = 8 if level else 0
        count = 2 if kind == "border" else inner
        shapes = [near((tiles, count, cols, cm)), near((-(-tiles * count // 8) * 8, cm))]
        return shapes + ([near((tiles, cols + room, cm)), near((tiles, cols, cm))] if kind == "border" else [])

    def reduce_call(kind, level, weights, before):
        return call(
            functools.partial(reduce_kernel, kind, rows), "reduce_" + kind,
            [(held, VMEM)] + [(a, VMEM) for a in weights] + [(before, ANY)],
            reduced_shapes(kind, 0), flops=3 * cells * c * cm, moved=4 * cells * c // 2,
        )

    def scratch(kind):
        count = 2 if kind == "border" else inner
        return [
            pltpu.VMEM((tiles, rows + 2, cols + 2 * PAD, cm), F32),
            pltpu.VMEM((tiles * count * cols, 9 * cm), BF16),
            pltpu.VMEM((tiles * count * cols, 9 * cm), BF16),
        ]

    def halos(msg_a, msg_b, swapped, level):
        axes = ("strip", "section")
        if level:
            shape = near((tiles, cols + 8, cm))
            (msg_a,) = call(append_kernel, "append", [(msg_a, VMEM), (swapped, VMEM)], [shape], aliases={0: 0})
        else:
            msg_a, _ = lax.optimization_barrier((msg_a, swapped))
        return lax.ppermute(msg_a, axes, pairs(0, level)), lax.ppermute(msg_b, axes, pairs(1, level))

    def with_corners(halo, before, count):
        args = [(a, VMEM) for a in halo[1::-1][:count]] + [(a, ANY) for a in before]
        shape = near((-(-count * tiles // 8) * 8, cm))
        (corners,) = call(functools.partial(corner_kernel, count), "corners", args, [shape])
        return halo + (swap(corners), corners)

    def block_call(kind, level, x, sent, weights, next_weights, before, halo=None):
        last = level == sections - 1
        (r_border, edge_border), (r_inner, edge_inner) = sent
        args = [(x, VMEM)]
        args += [(a, VMEM) for a in (r_border, r_inner, edge_border, edge_inner)]
        if kind == "border":
            args += [(a, VMEM) for a in halo[:3]]
        args += [(a, VMEM) for a in weights]
        if not last:
            args += [(a, VMEM) for a in next_weights]
        args.append((before, VMEM if last and kind == "border" else ANY))
        count = 2 if kind == "border" else inner
        more, out_specs, aliases, held_out = scratch(kind), None, None, near((tiles, count, c, cols))
        if last:
            held_out = near(flat.shape)
        outs = [held_out] + ([] if last else reduced_shapes(kind, level + 1))
        if last and kind == "border":
            outs = [pltpu.HBM(flat.shape, F32), held_out]
            out_specs = [ANY, VMEM]
            aliases = {len(args) - 1: 1}
            more.append(pltpu.SemaphoreType.DMA((tiles,)))
        return call(
            functools.partial(block_kernel, kind, rows, level, last), "block_" + kind, args, outs, more,
            flops=3 * cells * (13 if last else 17) * cm * cm, moved=4 * cells * c, out_specs=out_specs, aliases=aliases,
        )

    weights = reduce_weights(0)
    border = reduce_call("border", 0, weights, first)
    edges = swap(border[1])
    halo = halos(border[2], border[3], edges, 0)
    own = prepare_own(border[1])
    inside = reduce_call("inner", 0, weights, border[1])
    sent = ((border[0], edges), (inside[0], swap(inside[1])))
    halo = with_corners(halo, (own[4], sent[0][1], sent[1][1]), 2)
    x_border = x_inner = held
    for level in range(sections):
        last = level == sections - 1
        terms = weights[1]
        rest_of = tuple(rest_weights(level, terms)) + (terms,)
        if level > 0:
            sent = ((border[0], edges), (inside[0], swap(inside[1])))
        if last:
            (part,) = block_call("inner", level, x_inner, sent, rest_of, None, first)
            if level > 0:
                halo = with_corners(halo, (inside[1],), 1)
            whole = block_call("border", level, x_border, sent, rest_of, None, part, halo)[0]
        else:
            weights = reduce_weights(level + 1)
            x_border, *border = block_call("border", level, x_border, sent, rest_of, weights, first, halo)
            edges = swap(border[1])
            halo = halos(border[2], border[3], edges, level + 1)
            x_inner, *inside = block_call("inner", level, x_inner, sent, rest_of, weights, x_border)
            if level + 1 < sections - 1:
                halo = with_corners(halo, (inside[1],), 1)
    return whole.reshape(1, tiles, c, rows, cols)


def solution(mesh):
    in_specs = (
        P("groups", None, "strip", "col"),
        P("section", None, None),
        P("section", None, None, None),
        P("section", None, None),
        P("section", None, None),
        P("section", None, None),
        P("section", None),
        P("section", None),
    )
    out_specs = P("section", "groups", None, "strip", "col")
    return jax.shard_map(
        on_device, mesh=mesh, in_specs=in_specs, out_specs=out_specs, check_vma=False
    )
```

```python
import functools

import jax
import jax.numpy as jnp
from jax import lax
from jax.experimental import pallas as pl
from jax.experimental.pallas import tpu as pltpu
from jax.sharding import PartitionSpec as P

F32 = jnp.float32
BF16 = jnp.bfloat16
PAD = 8


def split(value):
    high = value.astype(BF16)
    return high, (value - high.astype(F32)).astype(BF16)


def dot(left, right):
    return jnp.dot(left, right, preferred_element_type=F32)


def dot_nt(left, right):
    return lax.dot_general(left, right, (((1,), (1,)), ((), ())), preferred_element_type=F32)


def first_core():
    return lax.axis_index("col") == 0


def even_strip(level):
    return lax.axis_index("strip") % 2 == (1 if level else 0)


def column_of(row):
    return jnp.concatenate(
        [
            jnp.transpose(jnp.broadcast_to(row[:, at : at + 128], (128, 128)))
            for at in range(0, row.shape[1], 128)
        ],
        axis=0,
    )


def pack_first_kernel(
    w_reduce, gain_mid, bias_mid, gain_out, bias_out, first, gain_held, bias_held, gain_row, bias_row, sem
):
    half = w_reduce.shape[1] // 2
    cm = gain_mid.shape[2]
    low = pl.multiple_of(lax.axis_index("col") * half, half)
    moves = [
        (w_reduce.at[0, pl.ds(low, half), :], first.at[:half, :]),
        (gain_mid.at[0], gain_held),
        (bias_mid.at[0], bias_held),
        (gain_out, gain_row),
        (bias_out, bias_row),
    ]
    copies = [pltpu.make_async_copy(here, there, sem.at[i]) for i, (here, there) in enumerate(moves)]
    for copy in copies:
        copy.start()
    first[half : half + 8, :] = jnp.zeros((8, first.shape[1]), F32)
    for copy in copies:
        copy.wait()
    for i in range(2):
        first[half : half + 1, i * cm : (i + 1) * cm] = gain_held[i : i + 1, :]
        first[half : half + 1, (2 + i) * cm : (3 + i) * cm] = bias_held[i : i + 1, :]
    first[half + 1 : half + 2, :] = gain_row[...]
    first[half + 2 : half + 3, :] = bias_row[...]


def pack_rest_kernel(w_spatial, w_expand, before, rest, sem):
    half = w_spatial.shape[2] // 2
    wide = w_expand.shape[1] // 2
    low = pl.multiple_of(lax.axis_index("col") * half, half)
    at = pl.multiple_of(lax.axis_index("col") * wide, wide)
    moves = [(w_expand.at[0, pl.ds(at, wide), :], rest.at[9 * half :, :])]
    for tap in range(9):
        moves.append((w_spatial.at[0, tap, pl.ds(low, half), :], rest.at[tap * half : (tap + 1) * half, :]))
    copies = [pltpu.make_async_copy(here, there, sem.at[i]) for i, (here, there) in enumerate(moves)]
    for copy in copies:
        copy.start()
    for copy in copies:
        copy.wait()


def fetch_kernel(x, w_reduce, before, x_held, w_held, sem):
    copies = [pltpu.make_async_copy(x.at[t], x_held.at[t], sem.at[t]) for t in range(x.shape[0])]
    copies.append(pltpu.make_async_copy(w_reduce.at[0], w_held, sem.at[x.shape[0]]))
    for copy in copies:
        copy.start()
    for copy in copies:
        copy.wait()


def corner_kernel(count, *refs):
    out = refs[-1]
    first = first_core()
    tiles = refs[0].shape[0]
    cols = refs[0].shape[1]
    out[...] = jnp.zeros_like(out)
    for i in range(count):
        for tile in range(tiles):
            side = jnp.where(first, refs[i][tile, cols - 1 : cols, :], refs[i][tile, 0:1, :])
            out[i * tiles + tile : i * tiles + tile + 1, :] = side


def append_kernel(msg, edges, out):
    even = even_strip(1)
    tiles = msg.shape[0]
    at = msg.shape[1] - 8
    for tile in range(tiles):
        out[tile, at : at + 1, :] = jnp.where(
            even, edges[2 * tile + 1 : 2 * tile + 2, :], edges[2 * tile : 2 * tile + 1, :]
        )


def store_reduce(w_high, at, rows):
    cm = w_high.shape[0] // 2
    high, low = split(rows)
    w_high[at : at + rows.shape[0], :] = high
    w_high[cm + at : cm + at + rows.shape[0], :] = low


def store_rest(tap_rows, expand_rows, gain_out, w_spatial, w_expand):
    cm = w_expand.shape[1] // 3
    for tap in range(9):
        high, low = split(jnp.transpose(tap_rows(tap)))
        w_spatial[tap * cm : (tap + 1) * cm, :cm] = high
        w_spatial[tap * cm : (tap + 1) * cm, cm:] = low
    high, low = split(expand_rows * column_of(gain_out))
    w_expand[:, :cm] = high
    w_expand[:, cm : 2 * cm] = low
    w_expand[:, 2 * cm :] = high


def prepare_own_kernel(w_reduce, w_spatial, w_expand, first, before, out_reduce, out_spatial, out_expand, out_shift, out_terms):
    half = w_reduce.shape[0] // 2
    store_reduce(out_reduce, 0, w_reduce[...])
    terms = first[half : half + 8, :]
    out_terms[...] = terms
    out_shift[...] = column_of(terms[2:3, :])
    store_rest(lambda tap: w_spatial[0, tap], w_expand[0], terms[1:2, :], out_spatial, out_expand)


def prepare_reduce_kernel(level, mine, other, w_reduce, first, out_reduce, out_terms):
    half = mine.shape[0] - 8

    @pl.when(lax.axis_index("section") == level)
    def _():
        store_reduce(out_reduce, 0, w_reduce[...])
        out_terms[...] = first[half:, :]

    @pl.when(lax.axis_index("section") != level)
    def _():
        out_terms[...] = mine[half:, :]
        for core in range(2):

            @pl.when(lax.axis_index("col") == core)
            def _(core=core):
                store_reduce(out_reduce, core * half, mine[:half, :])
                store_reduce(out_reduce, (1 - core) * half, other[:half, :])


def prepare_rest_kernel(
    level, mine, other, terms, own_spatial, own_expand, own_shift, out_spatial, out_expand, out_shift
):
    cm = own_expand.shape[1] // 3
    half, wide = cm // 2, own_expand.shape[0] // 2

    @pl.when(lax.axis_index("section") == level)
    def _():
        out_spatial[...] = own_spatial[...]
        out_expand[...] = own_expand[...]
        out_shift[...] = own_shift[...]

    @pl.when(lax.axis_index("section") != level)
    def _():
        out_shift[...] = column_of(terms[2:3, :])
        for core in range(2):

            @pl.when(lax.axis_index("col") == core)
            def _(core=core):
                low, up = (mine, other) if core == 0 else (other, mine)

                def tap_rows(tap):
                    at = slice(tap * half, (tap + 1) * half)
                    return jnp.concatenate([low[at, :], up[at, :]], axis=0)

                expand = jnp.concatenate([low[9 * half :, :], up[9 * half :, :]], axis=0)
                store_rest(tap_rows, expand, terms[1:2, :], out_spatial, out_expand)


def members(kind, rows):
    return (0, rows - 1) if kind == "border" else tuple(range(1, rows - 1))


def reduce_step(level, tile, field, w_reduce, terms, r_out, edge, msgs):
    cm = w_reduce.shape[0] // 2
    count, cols = r_out.shape[1:3]
    high, low = split(field)
    both = dot(w_reduce[...], high)
    total = both[:cm] + both[cm:] + dot(w_reduce[:cm, :], low)
    gain, shift = terms[0:1, 0:cm], terms[0:1, 2 * cm : 3 * cm]
    even, first = even_strip(level), first_core()
    turned = []
    for j in range(count):
        part = jnp.maximum(jnp.transpose(total[:, j * cols : (j + 1) * cols]) * gain + shift, 0.0)
        r_out[tile, j] = part
        at = tile * count + j
        edge[at : at + 1, :] = jnp.where(first, part[cols - 1 : cols, :], part[0:1, :])
        turned.append(part)
    if msgs:
        msgs[0][tile, :cols, :] = jnp.where(even, turned[-1], turned[0])
        if msgs[0].shape[1] > cols:
            msgs[0][tile, cols:, :] = jnp.zeros((msgs[0].shape[1] - cols, cm), F32)
        msgs[1][tile] = jnp.where(even, turned[0], turned[-1])


def field_rows(x, kind, rows, tile, j):
    if len(x.shape) == 3:
        return x[tile, pl.ds(members(kind, rows)[j], x.shape[1] // rows, stride=rows), :]
    return x[tile, j]


def reduce_kernel(kind, rows, x, w_reduce, terms, before, r_out, edge, *msgs):
    edge[...] = jnp.zeros_like(edge)
    count = r_out.shape[1]
    for tile in range(x.shape[0]):
        field = jnp.concatenate([field_rows(x, kind, rows, tile, j) for j in range(count)], axis=1)
        reduce_step(0, tile, field, w_reduce, terms, r_out, edge, msgs)


def block_kernel(kind, rows, level, last, *refs):
    refs = list(refs)

    def take(n):
        taken, refs[:n] = refs[:n], []
        return taken

    border = kind == "border"
    x, r_border, r_inner, edge_border, edge_inner = take(5)
    if border:
        halo_a, halo_b, corners = take(3)
    w_spatial, w_expand, shift_out, terms = take(4)
    if not last:
        next_reduce, next_terms = take(2)
    if last and border:
        take(1)
    else:
        take(1)
    outs = take(2 if last and border else 1)
    if not last:
        r_out, edge_out = take(2)
        msgs = take(2) if border else []
        edge_out[...] = jnp.zeros_like(edge_out)
    padded, taps_high, taps_low = take(3)
    tiles, _, cols, cm = r_border.shape
    chosen = members(kind, rows)
    count = len(chosen)
    inner = members("inner", rows)
    even, first = even_strip(level), first_core()
    gain, shift = terms[0:1, cm : 2 * cm], terms[0:1, 3 * cm : 4 * cm]
    keep = lax.axis_index("section") >= level

    def row_and_side(tile, i):
        if i in (-1, rows):
            from_a = even if i == rows else jnp.logical_not(even)
            side_b = corners[tile : tile + 1, :]
            side_a = halo_a[tile, cols : cols + 1, :] if level else corners[tiles + tile : tiles + tile + 1, :]
            return jnp.where(from_a, halo_a[tile, :cols, :], halo_b[tile]), jnp.where(from_a, side_a, side_b)
        if i in (0, rows - 1):
            j = 0 if i == 0 else 1
            return r_border[tile, j], edge_border[2 * tile + j : 2 * tile + j + 1, :]
        j = inner.index(i)
        at = tile * len(inner) + j
        return r_inner[tile, j], edge_inner[at : at + 1, :]

    span = count * cols
    group = 2 if last and border and tiles % 2 == 0 else tiles
    for g in range(0, tiles, group):
        for tile in range(g, g + group):
            for i in sorted({r + p for r in chosen for p in (-1, 0, 1)}):
                field, side = row_and_side(tile, i)
                slot = padded.at[tile, i + 1]
                slot[PAD : PAD + cols, :] = field
                slot[PAD - 1 : PAD, :] = jnp.where(first, 0.0, side)
                slot[PAD + cols : PAD + cols + 1, :] = jnp.where(first, side, 0.0)
                for q in range(3):
                    high, low = split(field if q == 1 else slot[PAD - 1 + q : PAD - 1 + q + cols, :])
                    for j, r in enumerate(chosen):
                        p = i - r + 1
                        if 0 <= p <= 2:
                            lanes = slice((3 * p + q) * cm, (3 * p + q + 1) * cm)
                            at = (tile * count + j) * cols
                            taps_high[at : at + cols, lanes] = high
                            taps_low[at : at + cols, lanes] = low
        at = slice(g * span, (g + group) * span)
        both = dot(taps_high[at, :], w_spatial[...])
        spatial = both[:, :cm] + both[:, cm:] + dot(taps_low[at, :], w_spatial[:, :cm])
        high, low = split(jnp.maximum(spatial * gain + shift, 0.0))
        middle = jnp.concatenate([high, high, low], axis=1)
        for tile in range(g, g + group):
            k = tile - g
            branch = dot_nt(w_expand[...], middle[k * span : (k + 1) * span])
            after = []
            for j in range(count):
                before = field_rows(x, kind, rows, tile, j)
                new = jnp.maximum(before + branch[:, j * cols : (j + 1) * cols] + shift_out[...], 0.0)
                after.append(jnp.where(keep, new, before) if level else new)
                if last:
                    whole = outs[-1]
                    whole[tile, pl.ds(chosen[j], whole.shape[1] // rows, stride=rows), :] = after[j]
                else:
                    outs[0][tile, j] = after[j]
            if not last:
                field = jnp.concatenate(after, axis=1)
                reduce_step(level + 1, tile, field, next_reduce, next_terms, r_out, edge_out, msgs)
            if last and border:
                sem = refs[0]
                pltpu.make_async_copy(outs[1].at[tile], outs[0].at[tile], sem.at[tile]).start()
    if last and border:
        sem = refs[0]
        for tile in range(tiles):
            pltpu.make_async_copy(outs[1].at[tile], outs[0].at[tile], sem.at[tile]).wait()


VMEM = pl.BlockSpec(memory_space=pltpu.VMEM)
ANY = pl.BlockSpec(memory_space=pl.ANY)
HBM = pl.BlockSpec(memory_space=pl.ANY)
FAR = pl.BlockSpec(memory_space=pltpu.VMEM)


def near(shape, dtype=F32):
    return pltpu.VMEM(shape, dtype)


def call(kernel, name, args, outs, scratch=(), flops=0, moved=0, specs=None, out_specs=None, aliases=None):
    held = {id(VMEM): pltpu.VMEM, id(HBM): pltpu.HBM, id(FAR): pltpu.HBM}
    arrays = [pltpu.with_memory_space_constraint(a, held[id(s)]) if id(s) in held else a for a, s in args]
    return pl.pallas_call(
        kernel,
        name=name,
        in_specs=[spec for _, spec in args],
        out_specs=out_specs or [VMEM] * len(outs),
        out_shape=outs,
        scratch_shapes=list(scratch),
        input_output_aliases=aliases or {},
        compiler_params=pltpu.CompilerParams(vmem_limit_bytes=16 * 2**20),
        cost_estimate=pl.CostEstimate(flops=flops, bytes_accessed=moved, transcendentals=0),
    )(*arrays)


def on_device(x_in, w_reduce, w_spatial, w_expand, gain_mid, bias_mid, gain_out, bias_out):
    sections = lax.axis_size("section")
    strips = lax.axis_size("strip")
    section = lax.axis_index("section")
    tiles, c, rows, cols = x_in.shape
    cm = w_reduce.shape[1]
    half, wide = cm // 2, c // 2
    inner = rows - 2
    cells = tiles * rows * cols

    def swap(array):
        return lax.ppermute(array, "col", [(0, 1), (1, 0)])

    def from_section(array, level):
        total = None
        for step in range(1, sections - level):
            sent = lax.ppermute(array, "section", [(i, i + step) for i in range(sections - step)])
            total = sent if total is None else jnp.where(section - level == step, sent, total)
        return total

    def pairs(start, level):
        found = []
        for i in range(start, strips - 1, 2):
            for j in range(level, sections):
                above, below = i * sections + j, (i + 1) * sections + j
                found += [(above, below), (below, above)]
        return found

    (first,) = call(
        pack_first_kernel, "pack_first", [(a, HBM) for a in (w_reduce, gain_mid, bias_mid, gain_out, bias_out)],
        [near((half + 8, c))],
        [pltpu.VMEM((2, cm), F32)] * 2 + [pltpu.VMEM((1, c), F32)] * 2 + [pltpu.SemaphoreType.DMA((5,))],
        moved=4 * half * c,
    )
    first_sent = [from_section(first, level) for level in range(sections - 1)]
    flat = x_in.reshape(tiles, c * rows, cols)
    held, w_held = call(
        fetch_kernel, "fetch", [(flat, HBM), (w_reduce, HBM), (first, ANY)], [near(flat.shape), near((cm, c))],
        [pltpu.SemaphoreType.DMA((tiles + 1,))], moved=4 * cells * c,
    )
    (rest,) = call(
        pack_rest_kernel, "pack_rest", [(w_spatial, HBM), (w_expand, HBM), (w_held, ANY)],
        [near((9 * half + wide, cm))], [pltpu.SemaphoreType.DMA((10,))], moved=4 * (9 * half + wide) * cm,
    )
    rest_sent = [from_section(rest, level) for level in range(sections - 1)]
    rest_shapes = [near((9 * cm, 2 * cm), BF16), near((c, 3 * cm), BF16), near((c, 128))]
    first_sent, held, w_held, _ = lax.optimization_barrier((first_sent, held, w_held, rest))

    def prepare_own(before):
        return call(
            prepare_own_kernel, "prepare_own",
            [(w_held, VMEM), (w_spatial, FAR), (w_expand, FAR), (first, VMEM), (before, ANY)],
            [near((2 * cm, c), BF16)] + rest_shapes + [near((8, c))], moved=4 * cm * (2 * c + 9 * cm),
        )

    def reduce_weights(level):
        if level == sections - 1 and level > 0:
            return own[0], own[4]
        if sections == 1:
            return prepare_own(first)[::4]
        mine = first_sent[level]
        return call(
            functools.partial(prepare_reduce_kernel, level), "prepare_reduce",
            [(a, VMEM) for a in (mine, swap(mine), w_held, first)],
            [near((2 * cm, c), BF16), near((8, c))], moved=4 * cm * c,
        )

    def rest_weights(level, terms):
        if level == sections - 1:
            return own[1:4]
        mine, _ = lax.optimization_barrier((rest_sent[level], halo[3]))
        return call(
            functools.partial(prepare_rest_kernel, level), "prepare_rest",
            [(a, VMEM) for a in (mine, swap(mine), terms, *own[1:4])],
            rest_shapes, moved=4 * cm * (c + 9 * cm),
        )

    def reduced_shapes(kind, level):
        room = 8 if level else 0
        count = 2 if kind == "border" else inner
        shapes = [near((tiles, count, cols, cm)), near((-(-tiles * count // 8) * 8, cm))]
        return shapes + ([near((tiles, cols + room, cm)), near((tiles, cols, cm))] if kind == "border" else [])

    def reduce_call(kind, level, weights, before):
        return call(
            functools.partial(reduce_kernel, kind, rows), "reduce_" + kind,
            [(held, VMEM)] + [(a, VMEM) for a in weights] + [(before, ANY)],
            reduced_shapes(kind, 0), flops=3 * cells * c * cm, moved=4 * cells * c // 2,
        )

    def scratch(kind):
        count = 2 if kind == "border" else inner
        return [
            pltpu.VMEM((tiles, rows + 2, cols + 2 * PAD, cm), F32),
            pltpu.VMEM((tiles * count * cols, 9 * cm), BF16),
            pltpu.VMEM((tiles * count * cols, 9 * cm), BF16),
        ]

    def halos(msg_a, msg_b, swapped, level):
        axes = ("strip", "section")
        if level:
            shape = near((tiles, cols + 8, cm))
            (msg_a,) = call(append_kernel, "append", [(msg_a, VMEM), (swapped, VMEM)], [shape], aliases={0: 0})
        else:
            msg_a, _ = lax.optimization_barrier((msg_a, swapped))
        return (
            lax.ppermute(msg_a, axes, pairs(1 if level else 0, level)),
            lax.ppermute(msg_b, axes, pairs(0 if level else 1, level)),
        )

    def with_corners(halo, before, count):
        args = [(a, VMEM) for a in halo[1::-1][:count]] + [(a, ANY) for a in before]
        shape = near((-(-count * tiles // 8) * 8, cm))
        (corners,) = call(functools.partial(corner_kernel, count), "corners", args, [shape])
        return halo + (swap(corners), corners)

    def block_call(kind, level, x, sent, weights, next_weights, before, halo=None):
        last = level == sections - 1
        (r_border, edge_border), (r_inner, edge_inner) = sent
        args = [(x, VMEM)]
        args += [(a, VMEM) for a in (r_border, r_inner, edge_border, edge_inner)]
        if kind == "border":
            args += [(a, VMEM) for a in halo[:3]]
        args += [(a, VMEM) for a in weights]
        if not last:
            args += [(a, VMEM) for a in next_weights]
        args.append((before, VMEM if last and kind == "border" else ANY))
        count = 2 if kind == "border" else inner
        more, out_specs, aliases, held_out = scratch(kind), None, None, near((tiles, count, c, cols))
        if last:
            held_out = near(flat.shape)
        outs = [held_out] + ([] if last else reduced_shapes(kind, level + 1))
        if last and kind == "border":
            outs = [pltpu.HBM(flat.shape, F32), held_out]
            out_specs = [ANY, VMEM]
            aliases = {len(args) - 1: 1}
            more.append(pltpu.SemaphoreType.DMA((tiles,)))
        return call(
            functools.partial(block_kernel, kind, rows, level, last), "block_" + kind, args, outs, more,
            flops=3 * cells * (13 if last else 17) * cm * cm, moved=4 * cells * c, out_specs=out_specs, aliases=aliases,
        )

    weights = reduce_weights(0)
    border = reduce_call("border", 0, weights, first)
    edges = swap(border[1])
    halo = halos(border[2], border[3], edges, 0)
    own = prepare_own(border[1])
    inside = reduce_call("inner", 0, weights, border[1])
    sent = ((border[0], edges), (inside[0], swap(inside[1])))
    halo = with_corners(halo, (own[4], sent[0][1], sent[1][1]), 2)
    x_border = x_inner = held
    for level in range(sections):
        last = level == sections - 1
        terms = weights[1]
        rest_of = tuple(rest_weights(level, terms)) + (terms,)
        if level > 0:
            sent = ((border[0], edges), (inside[0], swap(inside[1])))
        if last:
            (part,) = block_call("inner", level, x_inner, sent, rest_of, None, first)
            if level > 0:
                halo = with_corners(halo, (inside[1],), 1)
            whole = block_call("border", level, x_border, sent, rest_of, None, part, halo)[0]
        else:
            weights = reduce_weights(level + 1)
            x_border, *border = block_call("border", level, x_border, sent, rest_of, weights, first, halo)
            edges = swap(border[1])
            halo = halos(border[2], border[3], edges, level + 1)
            x_inner, *inside = block_call("inner", level, x_inner, sent, rest_of, weights, x_border)
            if level + 1 < sections - 1:
                halo = with_corners(halo, (inside[1],), 1)
    return whole.reshape(1, tiles, c, rows, cols)


def solution(mesh):
    in_specs = (
        P("groups", None, "strip", "col"),
        P("section", None, None),
        P("section", None, None, None),
        P("section", None, None),
        P("section", None, None),
        P("section", None, None),
        P("section", None),
        P("section", None),
    )
    out_specs = P("section", "groups", None, "strip", "col")
    return jax.shard_map(
        on_device, mesh=mesh, in_specs=in_specs, out_specs=out_specs, check_vma=False
    )
```
